256 devices in a mesh: seq: 64 (over z_hi, y, x), ch: 4 (over z_lo, core).
Axes of the slice: x: 4, y: 4, z: 8 (z_hi: 4, z_lo: 2; z = z_hi * 2 + z_lo), core: 2. Of those that a mesh axis runs over, the one named last changes fastest.
Arguments:
- output_gate: bfloat16 [8192, 4096], P('seq', 'ch'), may hold values from -6 to 6
- input_gate: bfloat16 [8192, 4096], P('seq', 'ch'), may hold values from -6 to 6
- values_in: bfloat16 [8192, 4096], P('seq', 'ch'), may hold values from -6 to 6
- filters: bfloat16 [8192, 4096], P(None, ('seq', 'ch')), may hold values from -6 to 6
- cotangent: bfloat16 [8192, 4096], P('seq', 'ch'), may hold values from -6 to 6
Outputs:
- output: bfloat16 [8192, 4096], P('seq', 'ch')
- grad_output_gate: bfloat16 [8192, 4096], P('seq', 'ch')
- grad_input_gate: bfloat16 [8192, 4096], P('seq', 'ch')
- grad_values: bfloat16 [8192, 4096], P('seq', 'ch')
- grad_filters: float32 [8192, 4096], P(None, ('seq', 'ch'))
The draws below stay inside these ranges and needn't reach their ends.
All inputs are finite; a program needn't handle non-finite values.
Results may differ from the reference program's by a relative error of at most 0.0058.
Values may be sent and summed in bfloat16 or wider, within the bound.
No kernel may reach another device: no remote copies, remote signals or barrier semaphores. Data moves between devices by JAX's collectives and lax.ppermute only.
A program may use at most 64 MiB of HBM per device.

```python
import math
import jax
import jax.numpy as jnp
from jax import lax

D = 4096
SEQ = 8192


def block_scale(own_key, extent, split, smallest, high):
    loudness = 1.0
    for axis_at, blocks in split:
        steps = jax.random.uniform(jax.random.fold_in(jax.random.fold_in(own_key, 6), axis_at), (blocks,), jnp.float32, smallest / len(split), high / len(split))
        loudness = loudness * jnp.repeat(jnp.exp(steps), extent[axis_at] // blocks).reshape((-1,) + (1,) * (len(extent) - 1 - axis_at))
    return loudness


def gaussian(stream_key, extent, spread, most, shards=(), kind=jnp.bfloat16):
    level = block_scale(stream_key, extent, shards, -0.22, 0.18) if shards else 1.0
    result = jax.random.normal(stream_key, extent, jnp.float32) * spread * level
    return jnp.minimum(jnp.maximum(result, -most), most).astype(kind)


def setup_inputs(seed: int = 0) -> dict:
    key_of = jax.random.split(jax.random.key(seed), 6)
    output_gate = gaussian(key_of[0], (SEQ, D), 1.0, 6.0, ((0, 64), (1, 4)))
    input_gate = gaussian(key_of[1], (SEQ, D), 1.0, 6.0, ((0, 64), (1, 4)))
    values_in = gaussian(key_of[2], (SEQ, D), 1.0, 6.0, ((0, 64), (1, 4)))
    filters = gaussian(key_of[3], (SEQ, D), 1.0, 6.0, ((1, 256),))
    cotangent = gaussian(key_of[4], (SEQ, D), 1.0, 6.0, ((0, 64), (1, 4)))
    return {"output_gate": output_gate, "input_gate": input_gate, "values_in": values_in, "filters": filters, "cotangent": cotangent}


def channel_block(items):
    out_gate, in_gate, values_blk, taps_raw, cotan = items
    wide = jnp.float32
    narrow = jnp.bfloat16
    padded = 2 * SEQ
    filter_scale = 1.0 / math.sqrt(SEQ)
    mixed = (in_gate.astype(wide) * values_blk.astype(wide)).astype(narrow)
    mixed_f = lax.optimization_barrier(mixed).astype(wide)
    taps = taps_raw.astype(wide) * filter_scale
    mixed_spec = jnp.fft.rfft(mixed_f, n=padded, axis=0)
    taps_spec = jnp.fft.rfft(taps, n=padded, axis=0)
    conv = jnp.fft.irfft(taps_spec * mixed_spec, n=padded, axis=0)[:SEQ].astype(narrow)
    conv_f = lax.optimization_barrier(conv).astype(wide)
    output = (out_gate.astype(wide) * conv_f).astype(narrow)
    grad_out = (cotan.astype(wide) * conv_f).astype(narrow)
    gated = (cotan.astype(wide) * out_gate.astype(wide)).astype(narrow)
    gated_f = lax.optimization_barrier(gated).astype(wide)
    gated_spec = jnp.fft.rfft(gated_f, n=padded, axis=0)
    grad_mixed = jnp.fft.irfft(jnp.conj(taps_spec) * gated_spec, n=padded, axis=0)[:SEQ].astype(narrow)
    grad_mixed_f = lax.optimization_barrier(grad_mixed).astype(wide)
    grad_in = (grad_mixed_f * values_blk.astype(wide)).astype(narrow)
    grad_vals = (grad_mixed_f * in_gate.astype(wide)).astype(narrow)
    grad_taps = jnp.fft.irfft(jnp.conj(mixed_spec) * gated_spec, n=padded, axis=0)[:SEQ].astype(wide) * filter_scale
    return (output, grad_out, grad_in, grad_vals, grad_taps)

def reference(output_gate, input_gate, values_in, filters, cotangent):
    block_width = min(D, 256)
    block_count = D // block_width

    def split_blocks(array):
        return array.reshape(SEQ, block_count, block_width).transpose(1, 0, 2)

    def join_blocks(array):
        return array.transpose(1, 0, 2).reshape(SEQ, D)
    results = lax.map(channel_block, (split_blocks(output_gate), split_blocks(input_gate), split_blocks(values_in), split_blocks(filters), split_blocks(cotangent)))
    return (join_blocks(results[0]), join_blocks(results[1]), join_blocks(results[2]), join_blocks(results[3]), join_blocks(results[4]))
```

```python
import math

import jax
import jax.numpy as jnp
from jax import lax
from jax.experimental import pallas as pl
from jax.experimental.pallas import tpu as pltpu
from jax.sharding import PartitionSpec as P

LANES = 128
ROWS = 16
WIDE = jnp.float32
NARROW = jnp.bfloat16


def exchange_matrix():
    row = lax.broadcasted_iota(jnp.int32, (LANES, LANES), 0)
    col = lax.broadcasted_iota(jnp.int32, (LANES, LANES), 1)
    return (row + col == LANES - 1).astype(NARROW)


def gate_kernel(out_gate, in_gate, values, cotan, send):
    groups, per_group, _, owned, _ = send.shape
    mixed = (in_gate[...].astype(WIDE) * values[...].astype(WIDE)).astype(NARROW)
    gated = (cotan[...].astype(WIDE) * out_gate[...].astype(WIDE)).astype(NARROW)
    flipped = jnp.dot(exchange_matrix(), gated, preferred_element_type=WIDE)
    for which, array in enumerate((mixed.astype(WIDE), flipped)):
        turned = array.T.astype(NARROW).reshape(per_group, groups, owned, LANES)
        for g in range(groups):
            send[g, :, which] = turned[:, g]


def gates(out_gate, in_gate, values, cotan, seq_count, chan_count):
    width = out_gate.shape[1]
    groups = chan_count
    per_group = seq_count // chan_count
    owned = width // seq_count
    steps = 4
    block = pl.BlockSpec((LANES, width // steps), lambda i: (0, i))
    return pl.pallas_call(
        gate_kernel,
        grid=(steps,),
        in_specs=[block] * 4,
        out_specs=pl.BlockSpec((groups, per_group // steps, 2, owned, LANES), lambda i: (0, i, 0, 0, 0)),
        out_shape=jax.ShapeDtypeStruct((groups, per_group, 2, owned, LANES), NARROW),
        name="gate_products",
    )(out_gate, in_gate, values, cotan)


def toeplitz(load_block, matrix, blocks):
    lane = lax.broadcasted_iota(jnp.int32, (ROWS, LANES), 1)
    row = lax.broadcasted_iota(jnp.int32, (ROWS, LANES), 0)
    tiles = LANES // ROWS
    zero = jnp.zeros((ROWS, LANES), NARROW)
    turned_before = jnp.zeros((ROWS, LANES), WIDE)
    before = [zero] * tiles
    for q in range(blocks):
        source = jnp.broadcast_to(load_block(q), (ROWS, LANES))
        turned = pltpu.roll(source, 0, axis=1, stride=1, stride_axis=0)
        base = jnp.where(lane >= row, turned, turned_before).astype(NARROW)
        turned_before = turned
        now = []
        for k in range(tiles):
            piece = base if k == 0 else pltpu.roll(base, ROWS * k, axis=1)
            tile = base if k == 0 else jnp.where(lane >= ROWS * k, piece, before[k])
            matrix[pl.ds(LANES * q + ROWS * k, ROWS), :] = tile
            now.append(piece)
        before = now


def causal_product(shifted, matrix, blocks):
    height = blocks // ROWS
    rows = shifted.shape[1]
    depth = ROWS * LANES
    parts = []
    for step in range(height):
        left = shifted[0 : height - step].reshape((height - step) * rows, depth)
        product = jnp.dot(
            left, matrix[pl.ds(step * depth, depth), :], preferred_element_type=WIDE
        ).reshape(height - step, rows, LANES)
        for at in range(height - step):
            if step == 0:
                parts.append(product[at])
            else:
                parts[at + step] = parts[at + step] + product[at]
    return parts


def conv_kernel(
    scale, received, filters, send, grad_filters, signal, taps, back, grads, shifted, matrix
):
    blocks, _, owned, _ = received.shape
    height = blocks // ROWS
    pad = ROWS * owned
    for which in range(2):
        signal[which, pl.ds(0, pad), :] = jnp.zeros((pad, LANES), WIDE)
    for j in range(blocks):
        signal[0, pl.ds(pad + j * owned, owned), :] = received[j, 0].astype(WIDE)
        signal[1, pl.ds(pad + j * owned, owned), :] = received[blocks - 1 - j, 1].astype(WIDE)
    for q in range(blocks):
        taps[pl.ds(q * owned, owned), :] = filters[:, pl.ds(q * LANES, LANES)].astype(WIDE)

    def channel(c, carry):
        for which in range(2):
            for r in range(ROWS):
                rows = signal[which, pl.ds(c + (ROWS - r) * owned, blocks, stride=owned), :]
                rows = rows.astype(NARROW).reshape(height, ROWS, LANES)
                shifted[:, which, :, pl.ds(r * LANES, LANES)] = rows
        toeplitz(lambda q: taps[pl.ds(q * owned + c, 1), :], matrix, blocks)
        both = causal_product(
            shifted[...].reshape(height, 2 * ROWS, ROWS * LANES), matrix, blocks
        )
        for at in range(height):
            forth = (at * ROWS) * owned + c
            back[0, pl.ds(forth, ROWS, stride=owned), :] = both[at][:ROWS] * scale
            back[1, pl.ds(forth, ROWS, stride=owned), :] = both[at][ROWS:] * scale
        toeplitz(
            lambda q: signal[0, pl.ds(pad + q * owned + c, 1), :], matrix, blocks
        )
        grad = causal_product(shifted[:, 1], matrix, blocks)
        for at in range(height):
            grads[pl.ds((at * ROWS) * owned + c, ROWS, stride=owned), :] = grad[at] * scale
        return carry

    lax.fori_loop(0, owned, channel, 0)
    conv = back[0].reshape(blocks, owned, LANES).astype(NARROW)
    grad_mixed = back[1].reshape(blocks, owned, LANES).astype(NARROW)
    for j in range(blocks):
        send[j, 0] = conv[j]
        send[j, 1] = grad_mixed[blocks - 1 - j]
    grad_filters[...] = grads[...].reshape(blocks, owned, LANES).astype(NARROW)


def convolutions(received, filters, scale):
    blocks, _, owned, _ = received.shape
    length = blocks * LANES
    vmem = pl.BlockSpec(memory_space=pltpu.VMEM)
    return pl.pallas_call(
        lambda *refs: conv_kernel(scale, *refs),
        in_specs=[vmem, vmem],
        out_specs=[vmem, vmem],
        out_shape=[
            jax.ShapeDtypeStruct(received.shape, NARROW),
            jax.ShapeDtypeStruct((blocks, owned, LANES), NARROW),
        ],
        scratch_shapes=[
            pltpu.VMEM((2, (ROWS + blocks) * owned, LANES), WIDE),
            pltpu.VMEM((blocks * owned, LANES), WIDE),
            pltpu.VMEM((2, blocks * owned, LANES), WIDE),
            pltpu.VMEM((blocks * owned, LANES), WIDE),
            pltpu.VMEM((blocks // ROWS, 2, ROWS, ROWS * LANES), NARROW),
            pltpu.VMEM((length, LANES), NARROW),
        ],
        compiler_params=pltpu.CompilerParams(vmem_limit_bytes=32 * 1024 * 1024),
        name="convolutions",
    )(received, filters)


def result_kernel(out_gate, in_gate, values, cotan, received, output, grad_out, grad_in, grad_values):
    groups, per_group, _, owned, _ = received.shape
    turned = []
    for which in range(2):
        pieces = [received[g, :, which] for g in range(groups)]
        array = jnp.stack(pieces, axis=1).reshape(groups * per_group * owned, LANES)
        turned.append(array.astype(WIDE).T)
    conv = turned[0]
    grad_mixed = jnp.dot(
        exchange_matrix(), turned[1].astype(NARROW), preferred_element_type=WIDE
    )
    output[...] = (out_gate[...].astype(WIDE) * conv).astype(NARROW)
    grad_out[...] = (cotan[...].astype(WIDE) * conv).astype(NARROW)
    grad_in[...] = (grad_mixed * values[...].astype(WIDE)).astype(NARROW)
    grad_values[...] = (grad_mixed * in_gate[...].astype(WIDE)).astype(NARROW)


def results(out_gate, in_gate, values, cotan, received):
    groups, per_group, _, owned, _ = received.shape
    width = out_gate.shape[1]
    steps = 4
    block = pl.BlockSpec((LANES, width // steps), lambda i: (0, i))
    return pl.pallas_call(
        result_kernel,
        grid=(steps,),
        in_specs=[block] * 4
        + [pl.BlockSpec((groups, per_group // steps, 2, owned, LANES), lambda i: (0, i, 0, 0, 0))],
        out_specs=[block] * 4,
        out_shape=[jax.ShapeDtypeStruct(out_gate.shape, NARROW)] * 4,
        name="gate_results",
    )(out_gate, in_gate, values, cotan, received)


def filter_kernel(received, grad_filters):
    blocks, owned, _ = received.shape
    flat = received[...].reshape(blocks * owned, LANES)
    flipped = jnp.dot(flat, exchange_matrix(), preferred_element_type=WIDE)
    flipped = flipped.reshape(blocks, owned, LANES)
    for j in range(blocks):
        grad_filters[:, pl.ds(j * LANES, LANES)] = flipped[blocks - 1 - j]


def filter_results(received):
    blocks, owned, _ = received.shape
    return pl.pallas_call(
        filter_kernel,
        out_shape=jax.ShapeDtypeStruct((owned, blocks * LANES), WIDE),
        name="filter_results",
    )(received)


def per_device(output_gate, input_gate, values_in, filters, cotangent):
    seq_count = lax.axis_size("seq")
    chan_count = lax.axis_size("ch")
    per_group = seq_count // chan_count
    length, owned = filters.shape
    scale = 1.0 / math.sqrt(length)
    swap = []
    for s in range(seq_count):
        for c in range(chan_count):
            high, low = divmod(s, per_group)
            swap.append((s * chan_count + c, (c * per_group + low) * chan_count + high))
    filters_here = lax.ppermute(filters.T, ("seq", "ch"), swap)
    send = gates(output_gate, input_gate, values_in, cotangent, seq_count, chan_count)
    sections = send.reshape(seq_count, 2, owned, LANES)
    received = lax.all_to_all(sections, "seq", split_axis=0, concat_axis=0, tiled=True)
    back, grads = convolutions(received, filters_here, scale)
    grads_owned = lax.ppermute(grads, ("seq", "ch"), swap)
    returned = lax.all_to_all(back, "seq", split_axis=0, concat_axis=0, tiled=True)
    returned = returned.reshape(chan_count, per_group, 2, owned, LANES)
    grad_filters = filter_results(grads_owned).T
    output, grad_out, grad_in, grad_values = results(
        output_gate, input_gate, values_in, cotangent, returned
    )
    return (output, grad_out, grad_in, grad_values, grad_filters)


def solution(mesh):
    by_position = P("seq", "ch")
    by_channel = P(None, ("seq", "ch"))
    return jax.shard_map(
        per_device,
        mesh=mesh,
        in_specs=(by_position, by_position, by_position, by_channel, by_position),
        out_specs=(by_position, by_position, by_position, by_position, by_channel),
        check_vma=False,
    )
```

```python
import functools
import math

import jax
import jax.numpy as jnp
import numpy as np
from jax import lax
from jax.experimental import pallas as pl
from jax.experimental.pallas import tpu as pltpu
from jax.sharding import PartitionSpec as P

LANES = 128
TOGETHER = 2
WIDE = jnp.float32
NARROW = jnp.bfloat16


def exchange_matrix():
    row = lax.broadcasted_iota(jnp.int32, (LANES, LANES), 0)
    col = lax.broadcasted_iota(jnp.int32, (LANES, LANES), 1)
    return (row + col == LANES - 1).astype(NARROW)


def gate_kernel(out_gate, in_gate, values, cotan, send):
    groups, per_group, _, owned, _ = send.shape
    mixed = (in_gate[...].astype(WIDE) * values[...].astype(WIDE)).astype(NARROW)
    gated = (cotan[...].astype(WIDE) * out_gate[...].astype(WIDE)).astype(NARROW)
    flipped = jnp.dot(exchange_matrix(), gated, preferred_element_type=WIDE)
    for which, array in enumerate((mixed.astype(WIDE), flipped)):
        turned = array.T.astype(NARROW).reshape(per_group, groups, owned, LANES)
        for g in range(groups):
            send[g, :, which] = turned[:, g]


def gates(out_gate, in_gate, values, cotan, seq_count, chan_count):
    width = out_gate.shape[1]
    groups = chan_count
    per_group = seq_count // chan_count
    owned = width // seq_count
    steps = 4
    block = pl.BlockSpec((LANES, width // steps), lambda i: (0, i))
    return pl.pallas_call(
        gate_kernel,
        grid=(steps,),
        in_specs=[block] * 4,
        out_specs=pl.BlockSpec((groups, per_group // steps, 2, owned, LANES), lambda i: (0, i, 0, 0, 0)),
        out_shape=jax.ShapeDtypeStruct((groups, per_group, 2, owned, LANES), NARROW),
        name="gate_products",
    )(out_gate, in_gate, values, cotan)


def split(array):
    high = array.astype(NARROW)
    low = (array - high.astype(WIDE)).astype(NARROW)
    return high, low


def split_table(array):
    high = array.astype(NARROW)
    low = (array - high.astype(np.float64)).astype(NARROW)
    return high, low


def dft_tables(blocks):
    padded = LANES * LANES
    index = np.arange(LANES)
    angle = 2.0 * np.pi / LANES * (index[:, None] * index[None, :] % LANES)
    cos, sin = np.cos(angle), np.sin(angle)
    near_cos, near_sin = cos[:, :blocks], sin[:, :blocks]
    turn = 2.0 * np.pi / padded * (index[:, None] * index[None, :])

    def across(table, order):
        parts = split_table(table)
        return np.concatenate([parts[at] for at in order], axis=1)

    def down(table, order):
        parts = split_table(table)
        return np.concatenate([parts[at] for at in order], axis=0)

    return {
        "first": across(np.block([[near_cos, near_sin], [-near_sin, near_cos]]), (0, 1)),
        "first_real": across(np.block([[near_cos], [-near_sin]]), (0, 1)),
        "second": down(np.block([[cos, -sin], [sin, cos]]), (0, 0, 1)),
        "second_back": down(np.block([[cos, sin], [-sin, cos]]), (0, 0, 1)),
        "first_back": across(
            np.block([[near_cos.T, -near_sin.T], [near_sin.T, near_cos.T]]), (0, 0, 1)
        ),
        "first_back_imag": across(np.block([[near_sin.T, near_cos.T]]), (0, 0, 1)),
        "turn_cos": np.cos(turn).astype(np.float32),
        "turn_sin": np.sin(turn).astype(np.float32),
    }


def dot(left, right):
    return jnp.dot(left, right, preferred_element_type=WIDE)


def three_parts(real, imag, axis):
    real_high, real_low = split(real)
    imag_high, imag_low = split(imag)
    return jnp.concatenate(
        [real_high, imag_high, real_low, imag_low, real_high, imag_high], axis=axis
    )


def spectra(data, first, second, turn_cos, turn_sin):
    stacked = jnp.concatenate([jnp.concatenate([one, one], axis=0) for one in data], axis=1)
    sections = dot(first[...], stacked)
    out = []
    for at in range(len(data)):
        real = sections[:LANES, at * LANES : (at + 1) * LANES]
        imag = sections[LANES:, at * LANES : (at + 1) * LANES]
        turned_real = real * turn_cos[...] + imag * turn_sin[...]
        turned_imag = imag * turn_cos[...] - real * turn_sin[...]
        spectrum = dot(three_parts(turned_real, turned_imag, 1), second[...])
        out.append(spectrum)
    return out


def signals(spectrum, first_back, second_back, turn_cos, turn_sin):
    turned = []
    for real, imag in spectrum:
        part = dot(three_parts(real, imag, 1), second_back[...])
        real, imag = part[:, :LANES], part[:, LANES:]
        turned_real = real * turn_cos[...] - imag * turn_sin[...]
        turned_imag = imag * turn_cos[...] + real * turn_sin[...]
        turned.append(three_parts(turned_real, turned_imag, 0))
    result = dot(first_back[...], jnp.concatenate(turned, axis=1))
    return [result[:, at * LANES : (at + 1) * LANES] for at in range(len(spectrum))]


def spectrum_kernel(filters, first, second, turn_cos, turn_sin, spectrum, taps):
    owned = filters.shape[0]
    blocks = filters.shape[1] // LANES
    for q in range(blocks):
        taps[pl.ds(q * owned, owned), :] = filters[:, pl.ds(q * LANES, LANES)].astype(WIDE)

    def pair(at, carry):
        data = [
            taps[pl.ds(TOGETHER * at + c, blocks, stride=owned), :].astype(NARROW)
            for c in range(TOGETHER)
        ]
        found = spectra(data, first, second, turn_cos, turn_sin)
        for c in range(TOGETHER):
            spectrum[TOGETHER * at + c] = found[c]
        return carry

    lax.fori_loop(0, owned // TOGETHER, pair, 0)


def power_of_two(size):
    exponent = jnp.floor(jnp.log2(jnp.maximum(size, 1e-30)))
    down = jnp.exp2(-exponent).astype(NARROW).astype(WIDE)
    up = jnp.exp2(exponent).astype(NARROW).astype(WIDE)
    return down, up


def convolution_kernel(
    scale,
    received,
    filter_spectrum,
    first,
    second,
    first_back,
    second_back,
    turn_cos,
    turn_sin,
    send,
    own_spectrum,
    sizes,
    signal,
    back,
):
    blocks, _, owned, _ = received.shape
    for which in range(2):
        size = jnp.zeros((owned, LANES), WIDE)
        for j in range(blocks):
            size = jnp.maximum(size, jnp.abs(received[j, which].astype(WIDE)))
        size = jnp.broadcast_to(jnp.max(size, axis=1, keepdims=True), (owned, LANES))
        down, up = power_of_two(size)
        sizes[which] = up
        for j in range(blocks):
            at = j if which == 0 else blocks - 1 - j
            signal[which, pl.ds(at * owned, owned), :] = received[j, which].astype(WIDE) * down

    def pair(at, carry):
        data = []
        for c in range(TOGETHER):
            rows = [
                signal[which, pl.ds(TOGETHER * at + c, blocks, stride=owned), :].astype(NARROW)
                for which in range(2)
            ]
            data.append(jnp.concatenate(rows, axis=0))
        found = spectra(data, first, second, turn_cos, turn_sin)
        products = []
        for c in range(TOGETHER):
            own_spectrum[TOGETHER * at + c] = found[c]
            real, imag = found[c][:, :LANES], found[c][:, LANES:]
            taps_real = filter_spectrum[TOGETHER * at + c, :, :LANES]
            taps_imag = filter_spectrum[TOGETHER * at + c, :, LANES:]
            products.append(
                (real * taps_real - imag * taps_imag, real * taps_imag + imag * taps_real)
            )
        result = signals(products, first_back, second_back, turn_cos, turn_sin)
        for c in range(TOGETHER):
            for which in range(2):
                back[which, pl.ds(TOGETHER * at + c, blocks, stride=owned), :] = result[c][
                    which * blocks : (which + 1) * blocks
                ]
        return carry

    lax.fori_loop(0, owned // TOGETHER, pair, 0)
    for which in range(2):
        up = sizes[which] * scale
        for j in range(blocks):
            at = j if which == 0 else blocks - 1 - j
            send[at, which] = (back[which, pl.ds(j * owned, owned), :] * up).astype(NARROW)


def gradient_kernel(
    scale,
    own_spectrum,
    sizes,
    first_back_imag,
    second_back,
    turn_cos,
    turn_sin,
    grad_filters,
    grads,
):
    blocks, owned, _ = grad_filters.shape

    def pair(at, carry):
        squares = []
        for c in range(TOGETHER):
            real = own_spectrum[TOGETHER * at + c, :, :LANES]
            imag = own_spectrum[TOGETHER * at + c, :, LANES:]
            squares.append((0.5 * (real - imag) * (real + imag), real * imag))
        result = signals(squares, first_back_imag, second_back, turn_cos, turn_sin)
        for c in range(TOGETHER):
            grads[pl.ds(TOGETHER * at + c, blocks, stride=owned), :] = result[c]
        return carry

    lax.fori_loop(0, owned // TOGETHER, pair, 0)
    up = sizes[0] * sizes[1] * scale
    for j in range(blocks):
        grad_filters[j] = (grads[pl.ds(j * owned, owned), :] * up).astype(NARROW)


def in_vmem(count):
    return [pl.BlockSpec(memory_space=pltpu.VMEM)] * count


def params():
    return pltpu.CompilerParams(vmem_limit_bytes=32 * 1024 * 1024)


def filter_spectra(filters, tables):
    owned, length = filters.shape
    return pl.pallas_call(
        spectrum_kernel,
        in_specs=in_vmem(5),
        out_specs=in_vmem(1)[0],
        out_shape=jax.ShapeDtypeStruct((owned, LANES, 2 * LANES), WIDE),
        scratch_shapes=[pltpu.VMEM((length // LANES * owned, LANES), WIDE)],
        compiler_params=params(),
        name="filter_spectra",
    )(filters, tables["first_real"], tables["second"], tables["turn_cos"], tables["turn_sin"])


def convolutions(received, filter_spectrum, tables, scale):
    blocks, _, owned, _ = received.shape
    return pl.pallas_call(
        functools.partial(convolution_kernel, scale / (LANES * LANES)),
        in_specs=in_vmem(8),
        out_specs=in_vmem(3),
        out_shape=[
            jax.ShapeDtypeStruct(received.shape, NARROW),
            jax.ShapeDtypeStruct((owned, LANES, 2 * LANES), WIDE),
            jax.ShapeDtypeStruct((2, owned, LANES), WIDE),
        ],
        scratch_shapes=[
            pltpu.VMEM((2, blocks * owned, LANES), WIDE),
            pltpu.VMEM((2, blocks * owned, LANES), WIDE),
        ],
        compiler_params=params(),
        name="convolutions",
    )(
        received,
        filter_spectrum,
        tables["first"],
        tables["second"],
        tables["first_back"],
        tables["second_back"],
        tables["turn_cos"],
        tables["turn_sin"],
    )


def filter_gradients(own_spectrum, sizes, blocks, tables, scale):
    owned = own_spectrum.shape[0]
    return pl.pallas_call(
        functools.partial(gradient_kernel, scale / (LANES * LANES)),
        in_specs=in_vmem(6),
        out_specs=in_vmem(1)[0],
        out_shape=jax.ShapeDtypeStruct((blocks, owned, LANES), NARROW),
        scratch_shapes=[pltpu.VMEM((blocks * owned, LANES), WIDE)],
        compiler_params=params(),
        name="filter_gradients",
    )(
        own_spectrum,
        sizes,
        tables["first_back_imag"],
        tables["second_back"],
        tables["turn_cos"],
        tables["turn_sin"],
    )


def result_kernel(out_gate, in_gate, values, cotan, received, output, grad_out, grad_in, grad_values):
    groups, per_group, _, owned, _ = received.shape
    turned = []
    for which in range(2):
        pieces = [received[g, :, which] for g in range(groups)]
        array = jnp.stack(pieces, axis=1).reshape(groups * per_group * owned, LANES)
        turned.append(array.astype(WIDE).T)
    conv = turned[0]
    grad_mixed = jnp.dot(
        exchange_matrix(), turned[1].astype(NARROW), preferred_element_type=WIDE
    )
    output[...] = (out_gate[...].astype(WIDE) * conv).astype(NARROW)
    grad_out[...] = (cotan[...].astype(WIDE) * conv).astype(NARROW)
    grad_in[...] = (grad_mixed * values[...].astype(WIDE)).astype(NARROW)
    grad_values[...] = (grad_mixed * in_gate[...].astype(WIDE)).astype(NARROW)


def results(out_gate, in_gate, values, cotan, received):
    groups, per_group, _, owned, _ = received.shape
    width = out_gate.shape[1]
    steps = 4
    block = pl.BlockSpec((LANES, width // steps), lambda i: (0, i))
    return pl.pallas_call(
        result_kernel,
        grid=(steps,),
        in_specs=[block] * 4
        + [pl.BlockSpec((groups, per_group // steps, 2, owned, LANES), lambda i: (0, i, 0, 0, 0))],
        out_specs=[block] * 4,
        out_shape=[jax.ShapeDtypeStruct(out_gate.shape, NARROW)] * 4,
        name="gate_results",
    )(out_gate, in_gate, values, cotan, received)


def filter_kernel(received, grad_filters):
    blocks, owned, _ = received.shape
    flat = received[...].reshape(blocks * owned, LANES)
    flipped = jnp.dot(flat, exchange_matrix(), preferred_element_type=WIDE)
    flipped = flipped.reshape(blocks, owned, LANES)
    for j in range(blocks):
        grad_filters[:, pl.ds(j * LANES, LANES)] = flipped[blocks - 1 - j]


def filter_results(received):
    blocks, owned, _ = received.shape
    return pl.pallas_call(
        filter_kernel,
        out_shape=jax.ShapeDtypeStruct((owned, blocks * LANES), WIDE),
        name="filter_results",
    )(received)


def per_device(output_gate, input_gate, values_in, filters, cotangent):
    seq_count = lax.axis_size("seq")
    chan_count = lax.axis_size("ch")
    per_group = seq_count // chan_count
    length, owned = filters.shape
    scale = 1.0 / math.sqrt(length)
    swap = []
    for s in range(seq_count):
        for c in range(chan_count):
            high, low = divmod(s, per_group)
            swap.append((s * chan_count + c, (c * per_group + low) * chan_count + high))
    tables = {name: jnp.asarray(table) for name, table in dft_tables(seq_count).items()}
    filters_here = lax.ppermute(filters.T, ("seq", "ch"), swap)
    filter_spectrum = filter_spectra(filters_here, tables)
    send = gates(output_gate, input_gate, values_in, cotangent, seq_count, chan_count)
    sections = send.reshape(seq_count, 2, owned, LANES)
    received = lax.all_to_all(sections, "seq", split_axis=0, concat_axis=0, tiled=True)
    back, own_spectrum, sizes = convolutions(received, filter_spectrum, tables, scale)
    grads = filter_gradients(own_spectrum, sizes, seq_count, tables, scale)
    grads_owned = lax.ppermute(grads, ("seq", "ch"), swap)
    returned = lax.all_to_all(back, "seq", split_axis=0, concat_axis=0, tiled=True)
    returned = returned.reshape(chan_count, per_group, 2, owned, LANES)
    grad_filters = filter_results(grads_owned).T
    output, grad_out, grad_in, grad_values = results(
        output_gate, input_gate, values_in, cotangent, returned
    )
    return (output, grad_out, grad_in, grad_values, grad_filters)


def solution(mesh):
    by_position = P("seq", "ch")
    by_channel = P(None, ("seq", "ch"))
    return jax.shard_map(
        per_device,
        mesh=mesh,
        in_specs=(by_position, by_position, by_position, by_channel, by_position),
        out_specs=(by_position, by_position, by_position, by_position, by_channel),
        check_vma=False,
    )
```

```python
import functools
import math

import jax
import jax.numpy as jnp
import numpy as np
from jax import lax
from jax.experimental import pallas as pl
from jax.experimental.pallas import tpu as pltpu
from jax.sharding import PartitionSpec as P

LANES = 128
TOGETHER = 2
WIDE = jnp.float32
NARROW = jnp.bfloat16


def exchange_matrix():
    row = lax.broadcasted_iota(jnp.int32, (LANES, LANES), 0)
    col = lax.broadcasted_iota(jnp.int32, (LANES, LANES), 1)
    return (row + col == LANES - 1).astype(NARROW)


def gate_kernel(out_gate, in_gate, values, cotan, send):
    groups, per_group, _, owned, _ = send.shape
    mixed = (in_gate[...].astype(WIDE) * values[...].astype(WIDE)).astype(NARROW)
    gated = (cotan[...].astype(WIDE) * out_gate[...].astype(WIDE)).astype(NARROW)
    flipped = dot(gated.T, exchange_matrix()).astype(NARROW)
    for which, array in enumerate((mixed.T, flipped)):
        turned = array.reshape(per_group, groups, owned, LANES)
        for g in range(groups):
            send[g, :, which] = turned[:, g]


def gates(out_gate, in_gate, values, cotan, seq_count, chan_count):
    width = out_gate.shape[1]
    groups = chan_count
    per_group = seq_count // chan_count
    owned = width // seq_count
    steps = 2
    block = pl.BlockSpec((LANES, width // steps), lambda i: (0, i))
    return pl.pallas_call(
        gate_kernel,
        grid=(steps,),
        in_specs=[block] * 4,
        out_specs=pl.BlockSpec((groups, per_group // steps, 2, owned, LANES), lambda i: (0, i, 0, 0, 0)),
        out_shape=jax.ShapeDtypeStruct((groups, per_group, 2, owned, LANES), NARROW),
        cost_estimate=cost(2),
        name="gate_products",
    )(out_gate, in_gate, values, cotan)


def split(array):
    high = array.astype(NARROW)
    low = (array - high.astype(WIDE)).astype(NARROW)
    return high, low


def split_table(array):
    high = array.astype(NARROW)
    low = (array - high.astype(np.float64)).astype(NARROW)
    return high, low


def dft_tables(blocks):
    padded = LANES * LANES
    index = np.arange(LANES)
    angle = 2.0 * np.pi / LANES * (index[:, None] * index[None, :] % LANES)
    cos, sin = np.cos(angle), np.sin(angle)
    near_cos, near_sin = cos[:, :blocks], sin[:, :blocks]
    turn = 2.0 * np.pi / padded * (index[:, None] * index[None, :])

    def across(table, order):
        parts = split_table(table)
        return np.concatenate([parts[at] for at in order], axis=1)

    def down(table, order):
        parts = split_table(table)
        return np.concatenate([parts[at] for at in order], axis=0)

    return {
        "first": across(np.block([[near_cos, near_sin], [-near_sin, near_cos]]), (0, 1)),
        "first_real": across(np.block([[near_cos], [-near_sin]]), (0, 1)),
        "second": down(np.block([[cos, -sin], [sin, cos]]), (0, 0, 1)),
        "second_back": down(np.block([[cos, sin], [-sin, cos]]), (0, 0, 1)),
        "first_back": across(
            np.block([[near_cos.T, -near_sin.T], [near_sin.T, near_cos.T]]), (0, 0, 1)
        ),
        "first_back_imag": across(np.block([[near_sin.T, near_cos.T]]), (0, 0, 1)),
        "turn_cos": np.cos(turn).astype(np.float32),
        "turn_sin": np.sin(turn).astype(np.float32),
    }


def dot(left, right):
    return jnp.dot(left, right, preferred_element_type=WIDE)


def three_parts(real, imag, axis):
    real_high, real_low = split(real)
    imag_high, imag_low = split(imag)
    return jnp.concatenate(
        [real_high, imag_high, real_low, imag_low, real_high, imag_high], axis=axis
    )


def spectra(data, first, second, turn_cos, turn_sin):
    stacked = jnp.concatenate([jnp.concatenate([one, one], axis=0) for one in data], axis=1)
    sections = dot(first[...], stacked)
    out = []
    for at in range(len(data)):
        real = sections[:LANES, at * LANES : (at + 1) * LANES]
        imag = sections[LANES:, at * LANES : (at + 1) * LANES]
        turned_real = real * turn_cos[...] + imag * turn_sin[...]
        turned_imag = imag * turn_cos[...] - real * turn_sin[...]
        spectrum = dot(three_parts(turned_real, turned_imag, 1), second[...])
        out.append(spectrum)
    return out


def signals(spectrum, first_back, second_back, turn_cos, turn_sin):
    turned = []
    for real, imag in spectrum:
        part = dot(three_parts(real, imag, 1), second_back[...])
        real, imag = part[:, :LANES], part[:, LANES:]
        turned_real = real * turn_cos[...] - imag * turn_sin[...]
        turned_imag = imag * turn_cos[...] + real * turn_sin[...]
        turned.append(three_parts(turned_real, turned_imag, 0))
    result = dot(first_back[...], jnp.concatenate(turned, axis=1))
    return [result[:, at * LANES : (at + 1) * LANES] for at in range(len(spectrum))]


def spectrum_kernel(filters, first, second, turn_cos, turn_sin, spectrum, taps):
    owned = filters.shape[0]
    blocks = filters.shape[1] // LANES
    for q in range(blocks):
        taps[pl.ds(q * owned, owned), :] = filters[:, pl.ds(q * LANES, LANES)].astype(WIDE)

    def pair(at, carry):
        data = [
            taps[pl.ds(TOGETHER * at + c, blocks, stride=owned), :].astype(NARROW)
            for c in range(TOGETHER)
        ]
        found = spectra(data, first, second, turn_cos, turn_sin)
        for c in range(TOGETHER):
            spectrum[TOGETHER * at + c] = found[c]
        return carry

    lax.fori_loop(0, owned // TOGETHER, pair, 0)


def power_of_two(size):
    exponent = jnp.floor(jnp.log2(jnp.maximum(size, 1e-30)))
    down = jnp.exp2(-exponent).astype(NARROW).astype(WIDE)
    up = jnp.exp2(exponent).astype(NARROW).astype(WIDE)
    return down, up


def convolution_kernel(
    scale,
    received_far,
    spectrum_far,
    first_far,
    second_far,
    first_back_far,
    second_back_far,
    turn_cos_far,
    turn_sin_far,
    first_back_imag_far,
    send_far,
    grad_filters,
    received,
    filter_spectrum,
    first,
    second,
    first_back,
    second_back,
    turn_cos,
    turn_sin,
    first_back_imag,
    send,
    signal,
    back,
    grads,
    loaded,
    sent,
):
    blocks, _, owned, _ = received.shape
    far = (
        received_far,
        first_far,
        turn_cos_far,
        turn_sin_far,
        second_far,
        spectrum_far,
        second_back_far,
        first_back_far,
        first_back_imag_far,
    )
    near = (
        received,
        first,
        turn_cos,
        turn_sin,
        second,
        filter_spectrum,
        second_back,
        first_back,
        first_back_imag,
    )
    loads = [
        pltpu.make_async_copy(one, other, loaded.at[at])
        for at, (one, other) in enumerate(zip(far, near))
    ]
    for load in loads:
        load.start()
    loads[0].wait()
    ups = []
    for which in range(2):
        size = jnp.zeros((owned, LANES), WIDE)
        for j in range(blocks):
            size = jnp.maximum(size, jnp.abs(received[j, which].astype(WIDE)))
        size = jnp.broadcast_to(jnp.max(size, axis=1, keepdims=True), (owned, LANES))
        down, up = power_of_two(size)
        ups.append(up)
        for j in range(blocks):
            at = j if which == 0 else blocks - 1 - j
            signal[which, pl.ds(at * owned, owned), :] = received[j, which].astype(WIDE) * down
    for load in loads[1:]:
        load.wait()

    def pair(at, carry):
        data = []
        for c in range(TOGETHER):
            rows = [
                signal[which, pl.ds(TOGETHER * at + c, blocks, stride=owned), :].astype(NARROW)
                for which in range(2)
            ]
            data.append(jnp.concatenate(rows, axis=0))
        found = spectra(data, first, second, turn_cos, turn_sin)
        products = []
        squares = []
        for c in range(TOGETHER):
            real, imag = found[c][:, :LANES], found[c][:, LANES:]
            squares.append((0.5 * (real - imag) * (real + imag), real * imag))
            taps_real = filter_spectrum[TOGETHER * at + c, :, :LANES]
            taps_imag = filter_spectrum[TOGETHER * at + c, :, LANES:]
            products.append(
                (real * taps_real - imag * taps_imag, real * taps_imag + imag * taps_real)
            )
        result = signals(products, first_back, second_back, turn_cos, turn_sin)
        for c in range(TOGETHER):
            for which in range(2):
                back[which, pl.ds(TOGETHER * at + c, blocks, stride=owned), :] = result[c][
                    which * blocks : (which + 1) * blocks
                ]
        result = signals(squares, first_back_imag, second_back, turn_cos, turn_sin)
        for c in range(TOGETHER):
            grads[pl.ds(TOGETHER * at + c, blocks, stride=owned), :] = result[c]
        return carry

    lax.fori_loop(0, owned // TOGETHER, pair, 0)
    up = ups[0] * ups[1] * scale
    for j in range(blocks):
        grad_filters[j] = (grads[pl.ds(j * owned, owned), :] * up).astype(NARROW)
    up = [one * scale for one in ups]
    pieces = 4
    rows = blocks // pieces
    sends = []
    for piece in range(pieces):
        for at in range(piece * rows, (piece + 1) * rows):
            for which in range(2):
                j = at if which == 0 else blocks - 1 - at
                value = back[which, pl.ds(j * owned, owned), :] * up[which]
                send[at, which] = value.astype(NARROW)
        part = pl.ds(piece * rows, rows)
        sends.append(pltpu.make_async_copy(send.at[part], send_far.at[part], sent.at[piece]))
        sends[-1].start()
    for one in sends:
        one.wait()


def in_vmem(count):
    return [pl.BlockSpec(memory_space=pltpu.VMEM)] * count


def params(mebibytes=60):
    return pltpu.CompilerParams(vmem_limit_bytes=mebibytes * 1024 * 1024)


def cost(micros):
    return pl.CostEstimate(flops=int(micros * 1e9), bytes_accessed=1024, transcendentals=0)


def filter_spectra(filters, tables):
    owned, length = filters.shape
    return pl.pallas_call(
        spectrum_kernel,
        in_specs=in_vmem(5),
        out_specs=in_vmem(1)[0],
        out_shape=jax.ShapeDtypeStruct((owned, LANES, 2 * LANES), WIDE),
        scratch_shapes=[pltpu.VMEM((length // LANES * owned, LANES), WIDE)],
        compiler_params=params(),
        cost_estimate=cost(12),
        name="filter_spectra",
    )(filters, tables["first_real"], tables["second"], tables["turn_cos"], tables["turn_sin"])


def convolutions(received, filter_spectrum, tables, scale):
    blocks, _, owned, _ = received.shape
    operands = (
        received,
        filter_spectrum,
        tables["first"],
        tables["second"],
        tables["first_back"],
        tables["second_back"],
        tables["turn_cos"],
        tables["turn_sin"],
        tables["first_back_imag"],
    )
    far = pl.BlockSpec(memory_space=pl.ANY)
    return pl.pallas_call(
        functools.partial(convolution_kernel, scale / (LANES * LANES)),
        in_specs=[far] * len(operands),
        out_specs=[far] + in_vmem(1),
        out_shape=[
            jax.ShapeDtypeStruct(received.shape, NARROW),
            jax.ShapeDtypeStruct((blocks, owned, LANES), NARROW),
        ],
        scratch_shapes=[pltpu.VMEM(one.shape, one.dtype) for one in operands]
        + [
            pltpu.VMEM(received.shape, NARROW),
            pltpu.VMEM((2, blocks * owned, LANES), WIDE),
            pltpu.VMEM((2, blocks * owned, LANES), WIDE),
            pltpu.VMEM((blocks * owned, LANES), WIDE),
            pltpu.SemaphoreType.DMA((len(operands),)),
            pltpu.SemaphoreType.DMA((4,)),
        ],
        compiler_params=params(48),
        cost_estimate=cost(6),
        name="convolutions",
    )(*operands)


def result_kernel(out_gate, in_gate, values, cotan, received, output, grad_out, grad_in, grad_values):
    groups, per_group, _, owned, _ = received.shape
    turned = []
    for which in range(2):
        pieces = [received[g, :, which] for g in range(groups)]
        turned.append(jnp.stack(pieces, axis=1).reshape(groups * per_group * owned, LANES))
    conv = turned[0].T.astype(WIDE)
    grad_mixed = dot(turned[1], exchange_matrix()).astype(NARROW).T.astype(WIDE)
    output[...] = (out_gate[...].astype(WIDE) * conv).astype(NARROW)
    grad_out[...] = (cotan[...].astype(WIDE) * conv).astype(NARROW)
    grad_in[...] = (grad_mixed * values[...].astype(WIDE)).astype(NARROW)
    grad_values[...] = (grad_mixed * in_gate[...].astype(WIDE)).astype(NARROW)


def results(out_gate, in_gate, values, cotan, received):
    groups, per_group, _, owned, _ = received.shape
    width = out_gate.shape[1]
    steps = 2
    block = pl.BlockSpec((LANES, width // steps), lambda i: (0, i))
    return pl.pallas_call(
        result_kernel,
        grid=(steps,),
        in_specs=[block] * 4
        + [pl.BlockSpec((groups, per_group // steps, 2, owned, LANES), lambda i: (0, i, 0, 0, 0))],
        out_specs=[block] * 4,
        out_shape=[jax.ShapeDtypeStruct(out_gate.shape, NARROW)] * 4,
        compiler_params=params(48),
        cost_estimate=cost(2),
        name="gate_results",
    )(out_gate, in_gate, values, cotan, received)


def filter_kernel(received, grad_filters):
    blocks, owned, _ = received.shape
    flat = received[...].reshape(blocks * owned, LANES)
    flipped = dot(flat, exchange_matrix()).reshape(blocks, owned, LANES)
    for j in range(blocks):
        grad_filters[:, pl.ds(j * LANES, LANES)] = flipped[blocks - 1 - j]


def filter_results(received):
    blocks, owned, _ = received.shape
    return pl.pallas_call(
        filter_kernel,
        out_shape=jax.ShapeDtypeStruct((owned, blocks * LANES), WIDE),
        compiler_params=params(48),
        cost_estimate=cost(12),
        name="filter_results",
    )(received)


def per_device(output_gate, input_gate, values_in, filters, cotangent):
    seq_count = lax.axis_size("seq")
    chan_count = lax.axis_size("ch")
    per_group = seq_count // chan_count
    length, owned = filters.shape
    scale = 1.0 / math.sqrt(length)
    swap = []
    for s in range(seq_count):
        for c in range(chan_count):
            high, low = divmod(s, per_group)
            swap.append((s * chan_count + c, (c * per_group + low) * chan_count + high))
    tables = {name: jnp.asarray(table) for name, table in dft_tables(seq_count).items()}
    filters_here = lax.ppermute(filters.T, ("seq", "ch"), swap)
    filter_spectrum = filter_spectra(filters_here, tables)
    send = gates(output_gate, input_gate, values_in, cotangent, seq_count, chan_count)
    sections = send.reshape(seq_count, 2, owned, LANES)
    received = lax.all_to_all(sections, "seq", split_axis=0, concat_axis=0, tiled=True)
    back, grads = convolutions(received, filter_spectrum, tables, scale)
    grads_owned = lax.ppermute(grads, ("seq", "ch"), swap)
    returned = lax.all_to_all(back, "seq", split_axis=0, concat_axis=0, tiled=True)
    returned = returned.reshape(chan_count, per_group, 2, owned, LANES)
    grad_filters = filter_results(grads_owned).T
    output, grad_out, grad_in, grad_values = results(
        output_gate, input_gate, values_in, cotangent, returned
    )
    return (output, grad_out, grad_in, grad_values, grad_filters)


def solution(mesh):
    by_position = P("seq", "ch")
    by_channel = P(None, ("seq", "ch"))
    return jax.shard_map(
        per_device,
        mesh=mesh,
        in_specs=(by_position, by_position, by_position, by_channel, by_position),
        out_specs=(by_position, by_position, by_position, by_position, by_channel),
        check_vma=False,
    )
```

```python
import functools
import math

import jax
import jax.numpy as jnp
import numpy as np
from jax import lax
from jax.experimental import pallas as pl
from jax.experimental.pallas import tpu as pltpu
from jax.sharding import PartitionSpec as P

LANES = 128
TOGETHER = 8
WIDE = jnp.float32
NARROW = jnp.bfloat16


def exchange_matrix():
    row = lax.broadcasted_iota(jnp.int32, (LANES, LANES), 0)
    col = lax.broadcasted_iota(jnp.int32, (LANES, LANES), 1)
    return (row + col == LANES - 1).astype(NARROW)


def gate_kernel(out_gate, in_gate, values, cotan, send):
    groups, per_group, _, owned, _ = send.shape
    mixed = (in_gate[...].astype(WIDE) * values[...].astype(WIDE)).astype(NARROW)
    gated = (cotan[...].astype(WIDE) * out_gate[...].astype(WIDE)).astype(NARROW)
    flipped = dot(gated.T, exchange_matrix()).astype(NARROW)
    for which, array in enumerate((mixed.T, flipped)):
        turned = array.reshape(per_group, groups, owned, LANES)
        for g in range(groups):
            send[g, :, which] = turned[:, g]


def gates(out_gate, in_gate, values, cotan, seq_count, chan_count):
    width = out_gate.shape[1]
    groups = chan_count
    per_group = seq_count // chan_count
    owned = width // seq_count
    steps = 2
    block = pl.BlockSpec((LANES, width // steps), lambda i: (0, i))
    return pl.pallas_call(
        gate_kernel,
        grid=(steps,),
        in_specs=[block] * 4,
        out_specs=pl.BlockSpec((groups, per_group // steps, 2, owned, LANES), lambda i: (0, i, 0, 0, 0)),
        out_shape=jax.ShapeDtypeStruct((groups, per_group, 2, owned, LANES), NARROW),
        cost_estimate=cost(2),
        name="gate_products",
    )(out_gate, in_gate, values, cotan)


def split(array):
    high = array.astype(NARROW)
    low = (array - high.astype(WIDE)).astype(NARROW)
    return high, low


def split_table(array):
    high = array.astype(NARROW)
    low = (array - high.astype(np.float64)).astype(NARROW)
    return high, low


def dft_tables(blocks):
    padded = LANES * LANES
    index = np.arange(LANES)
    angle = 2.0 * np.pi / LANES * (index[:, None] * index[None, :] % LANES)
    cos, sin = np.cos(angle), np.sin(angle)
    near_cos, near_sin = cos[:, :blocks], sin[:, :blocks]
    turn = 2.0 * np.pi / padded * (index[:, None] * index[None, :])

    def across(table, order):
        parts = split_table(table)
        return np.concatenate([parts[at] for at in order], axis=1)

    def down(table, order):
        parts = split_table(table)
        return np.concatenate([parts[at] for at in order], axis=0)

    return {
        "first": across(np.block([[near_cos, near_sin], [-near_sin, near_cos]]), (0, 1)),
        "first_real": across(np.block([[near_cos], [-near_sin]]), (0, 1)),
        "second": down(np.block([[cos, -sin], [sin, cos]]), (0, 0, 1)),
        "second_back": down(np.block([[cos, sin], [-sin, cos]]), (0, 0, 1)),
        "first_back": across(
            np.block([[near_cos.T, -near_sin.T], [near_sin.T, near_cos.T]]), (0, 0, 1)
        ),
        "first_back_imag": across(np.block([[near_sin.T, near_cos.T]]), (0, 0, 1)),
        "turn_cos": np.cos(turn).astype(np.float32),
        "turn_sin": np.sin(turn).astype(np.float32),
    }


def dot(left, right):
    return jnp.dot(left, right, preferred_element_type=WIDE)


def three_parts(real, imag, axis):
    real_high, real_low = split(real)
    imag_high, imag_low = split(imag)
    return jnp.concatenate(
        [real_high, imag_high, real_low, imag_low, real_high, imag_high], axis=axis
    )


def spectra(data, first, second, turn_cos, turn_sin):
    stacked = jnp.concatenate([jnp.concatenate([one, one], axis=0) for one in data], axis=1)
    sections = dot(first[...], stacked)
    out = []
    for at in range(len(data)):
        real = sections[:LANES, at * LANES : (at + 1) * LANES]
        imag = sections[LANES:, at * LANES : (at + 1) * LANES]
        turned_real = real * turn_cos[...] + imag * turn_sin[...]
        turned_imag = imag * turn_cos[...] - real * turn_sin[...]
        spectrum = dot(three_parts(turned_real, turned_imag, 1), second[...])
        out.append(spectrum)
    return out


def signals(spectrum, first_back, second_back, turn_cos, turn_sin):
    turned = []
    for real, imag in spectrum:
        part = dot(three_parts(real, imag, 1), second_back[...])
        real, imag = part[:, :LANES], part[:, LANES:]
        turned_real = real * turn_cos[...] - imag * turn_sin[...]
        turned_imag = imag * turn_cos[...] + real * turn_sin[...]
        turned.append(three_parts(turned_real, turned_imag, 0))
    result = dot(first_back[...], jnp.concatenate(turned, axis=1))
    return [result[:, at * LANES : (at + 1) * LANES] for at in range(len(spectrum))]


def spectrum_kernel(filters, first, second, turn_cos, turn_sin, spectrum, taps):
    owned = filters.shape[0]
    blocks = filters.shape[1] // LANES
    for q in range(blocks):
        taps[pl.ds(q * owned, owned), :] = filters[:, pl.ds(q * LANES, LANES)].astype(WIDE)

    def pair(at, carry):
        data = [
            taps[pl.ds(TOGETHER * at + c, blocks, stride=owned), :].astype(NARROW)
            for c in range(TOGETHER)
        ]
        found = spectra(data, first, second, turn_cos, turn_sin)
        for c in range(TOGETHER):
            spectrum[TOGETHER * at + c] = found[c]
        return carry

    lax.fori_loop(0, owned // TOGETHER, pair, 0)


def power_of_two(size):
    exponent = jnp.floor(jnp.log2(jnp.maximum(size, 1e-30)))
    down = jnp.exp2(-exponent).astype(NARROW).astype(WIDE)
    up = jnp.exp2(exponent).astype(NARROW).astype(WIDE)
    return down, up


def convolution_kernel(
    scale,
    received_far,
    spectrum_far,
    first_far,
    second_far,
    first_back_far,
    second_back_far,
    turn_cos_far,
    turn_sin_far,
    first_back_imag_far,
    send_far,
    grad_filters,
    received,
    filter_spectrum,
    first,
    second,
    first_back,
    second_back,
    turn_cos,
    turn_sin,
    first_back_imag,
    send,
    signal,
    back,
    grads,
    loaded,
    sent,
):
    blocks, _, owned, _ = received.shape
    far = (
        received_far,
        first_far,
        turn_cos_far,
        turn_sin_far,
        second_far,
        spectrum_far,
        second_back_far,
        first_back_far,
        first_back_imag_far,
    )
    near = (
        received,
        first,
        turn_cos,
        turn_sin,
        second,
        filter_spectrum,
        second_back,
        first_back,
        first_back_imag,
    )
    loads = [
        pltpu.make_async_copy(one, other, loaded.at[at])
        for at, (one, other) in enumerate(zip(far, near))
    ]
    for load in loads:
        load.start()
    loads[0].wait()
    ups = []
    for which in range(2):
        size = jnp.zeros((owned, LANES), WIDE)
        for j in range(blocks):
            size = jnp.maximum(size, jnp.abs(received[j, which].astype(WIDE)))
        size = jnp.broadcast_to(jnp.max(size, axis=1, keepdims=True), (owned, LANES))
        down, up = power_of_two(size)
        ups.append(up)
        for j in range(blocks):
            at = j if which == 0 else blocks - 1 - j
            signal[which, pl.ds(at * owned, owned), :] = received[j, which].astype(WIDE) * down
    for load in loads[1:]:
        load.wait()

    def pair(at, carry):
        data = []
        for c in range(TOGETHER):
            rows = [
                signal[which, pl.ds(TOGETHER * at + c, blocks, stride=owned), :].astype(NARROW)
                for which in range(2)
            ]
            data.append(jnp.concatenate(rows, axis=0))
        found = spectra(data, first, second, turn_cos, turn_sin)
        products = []
        squares = []
        for c in range(TOGETHER):
            real, imag = found[c][:, :LANES], found[c][:, LANES:]
            squares.append((0.5 * (real - imag) * (real + imag), real * imag))
            taps_real = filter_spectrum[TOGETHER * at + c, :, :LANES]
            taps_imag = filter_spectrum[TOGETHER * at + c, :, LANES:]
            products.append(
                (real * taps_real - imag * taps_imag, real * taps_imag + imag * taps_real)
            )
        result = signals(products, first_back, second_back, turn_cos, turn_sin)
        for c in range(TOGETHER):
            for which in range(2):
                back[which, pl.ds(TOGETHER * at + c, blocks, stride=owned), :] = result[c][
                    which * blocks : (which + 1) * blocks
                ]
        result = signals(squares, first_back_imag, second_back, turn_cos, turn_sin)
        for c in range(TOGETHER):
            grads[pl.ds(TOGETHER * at + c, blocks, stride=owned), :] = result[c]
        return carry

    lax.fori_loop(0, owned // TOGETHER, pair, 0)
    up = ups[0] * ups[1] * scale
    for j in range(blocks):
        grad_filters[j] = (grads[pl.ds(j * owned, owned), :] * up).astype(NARROW)
    up = [one * scale for one in ups]
    pieces = 4
    rows = blocks // pieces
    sends = []
    for piece in range(pieces):
        for at in range(piece * rows, (piece + 1) * rows):
            for which in range(2):
                j = at if which == 0 else blocks - 1 - at
                value = back[which, pl.ds(j * owned, owned), :] * up[which]
                send[at, which] = value.astype(NARROW)
        part = pl.ds(piece * rows, rows)
        sends.append(pltpu.make_async_copy(send.at[part], send_far.at[part], sent.at[piece]))
        sends[-1].start()
    for one in sends:
        one.wait()


def in_vmem(count):
    return [pl.BlockSpec(memory_space=pltpu.VMEM)] * count


def params(mebibytes=60):
    return pltpu.CompilerParams(vmem_limit_bytes=mebibytes * 1024 * 1024)


def cost(micros):
    return pl.CostEstimate(flops=int(micros * 1e9), bytes_accessed=1024, transcendentals=0)


def filter_spectra(filters, tables):
    owned, length = filters.shape
    return pl.pallas_call(
        spectrum_kernel,
        in_specs=in_vmem(5),
        out_specs=in_vmem(1)[0],
        out_shape=jax.ShapeDtypeStruct((owned, LANES, 2 * LANES), WIDE),
        scratch_shapes=[pltpu.VMEM((length // LANES * owned, LANES), WIDE)],
        compiler_params=params(),
        cost_estimate=cost(12),
        name="filter_spectra",
    )(filters, tables["first_real"], tables["second"], tables["turn_cos"], tables["turn_sin"])


def convolutions(received, filter_spectrum, tables, scale):
    blocks, _, owned, _ = received.shape
    operands = (
        received,
        filter_spectrum,
        tables["first"],
        tables["second"],
        tables["first_back"],
        tables["second_back"],
        tables["turn_cos"],
        tables["turn_sin"],
        tables["first_back_imag"],
    )
    far = pl.BlockSpec(memory_space=pl.ANY)
    return pl.pallas_call(
        functools.partial(convolution_kernel, scale / (LANES * LANES)),
        in_specs=[far] * len(operands),
        out_specs=[far] + in_vmem(1),
        out_shape=[
            jax.ShapeDtypeStruct(received.shape, NARROW),
            jax.ShapeDtypeStruct((blocks, owned, LANES), NARROW),
        ],
        scratch_shapes=[pltpu.VMEM(one.shape, one.dtype) for one in operands]
        + [
            pltpu.VMEM(received.shape, NARROW),
            pltpu.VMEM((2, blocks * owned, LANES), WIDE),
            pltpu.VMEM((2, blocks * owned, LANES), WIDE),
            pltpu.VMEM((blocks * owned, LANES), WIDE),
            pltpu.SemaphoreType.DMA((len(operands),)),
            pltpu.SemaphoreType.DMA((4,)),
        ],
        compiler_params=params(50),
        cost_estimate=cost(6),
        name="convolutions",
    )(*operands)


def result_kernel(out_gate, in_gate, values, cotan, received, output, grad_out, grad_in, grad_values):
    groups, per_group, _, owned, _ = received.shape
    turned = []
    for which in range(2):
        pieces = [received[g, :, which] for g in range(groups)]
        turned.append(jnp.stack(pieces, axis=1).reshape(groups * per_group * owned, LANES))
    conv = turned[0].T.astype(WIDE)
    grad_mixed = dot(turned[1], exchange_matrix()).astype(NARROW).T.astype(WIDE)
    output[...] = (out_gate[...].astype(WIDE) * conv).astype(NARROW)
    grad_out[...] = (cotan[...].astype(WIDE) * conv).astype(NARROW)
    grad_in[...] = (grad_mixed * values[...].astype(WIDE)).astype(NARROW)
    grad_values[...] = (grad_mixed * in_gate[...].astype(WIDE)).astype(NARROW)


def results(out_gate, in_gate, values, cotan, received):
    groups, per_group, _, owned, _ = received.shape
    width = out_gate.shape[1]
    steps = 2
    block = pl.BlockSpec((LANES, width // steps), lambda i: (0, i))
    return pl.pallas_call(
        result_kernel,
        grid=(steps,),
        in_specs=[block] * 4
        + [pl.BlockSpec((groups, per_group // steps, 2, owned, LANES), lambda i: (0, i, 0, 0, 0))],
        out_specs=[block] * 4,
        out_shape=[jax.ShapeDtypeStruct(out_gate.shape, NARROW)] * 4,
        compiler_params=params(50),
        cost_estimate=cost(2),
        name="gate_results",
    )(out_gate, in_gate, values, cotan, received)


def filter_kernel(received, grad_filters):
    blocks, owned, _ = received.shape
    flat = received[...].reshape(blocks * owned, LANES)
    flipped = dot(flat, exchange_matrix()).reshape(blocks, owned, LANES)
    for j in range(blocks):
        grad_filters[:, pl.ds(j * LANES, LANES)] = flipped[blocks - 1 - j]


def filter_results(received):
    blocks, owned, _ = received.shape
    return pl.pallas_call(
        filter_kernel,
        out_shape=jax.ShapeDtypeStruct((owned, blocks * LANES), WIDE),
        compiler_params=params(50),
        cost_estimate=cost(12),
        name="filter_results",
    )(received)


def per_device(output_gate, input_gate, values_in, filters, cotangent):
    seq_count = lax.axis_size("seq")
    chan_count = lax.axis_size("ch")
    per_group = seq_count // chan_count
    length, owned = filters.shape
    scale = 1.0 / math.sqrt(length)
    swap = []
    for s in range(seq_count):
        for c in range(chan_count):
            high, low = divmod(s, per_group)
            swap.append((s * chan_count + c, (c * per_group + low) * chan_count + high))
    tables = {name: jnp.asarray(table) for name, table in dft_tables(seq_count).items()}
    filters_here = lax.ppermute(filters.T, ("seq", "ch"), swap)
    filter_spectrum = filter_spectra(filters_here, tables)
    send = gates(output_gate, input_gate, values_in, cotangent, seq_count, chan_count)
    sections = send.reshape(seq_count, 2, owned, LANES)
    received = lax.all_to_all(sections, "seq", split_axis=0, concat_axis=0, tiled=True)
    back, grads = convolutions(received, filter_spectrum, tables, scale)
    grads_owned = lax.ppermute(grads, ("seq", "ch"), swap)
    returned = lax.all_to_all(back, "seq", split_axis=0, concat_axis=0, tiled=True)
    returned = returned.reshape(chan_count, per_group, 2, owned, LANES)
    grad_filters = filter_results(grads_owned).T
    output, grad_out, grad_in, grad_values = results(
        output_gate, input_gate, values_in, cotangent, returned
    )
    return (output, grad_out, grad_in, grad_values, grad_filters)


def solution(mesh):
    by_position = P("seq", "ch")
    by_channel = P(None, ("seq", "ch"))
    return jax.shard_map(
        per_device,
        mesh=mesh,
        in_specs=(by_position, by_position, by_position, by_channel, by_position),
        out_specs=(by_position, by_position, by_position, by_position, by_channel),
        check_vma=False,
    )
```

```python
import functools
import math

import jax
import jax.numpy as jnp
import numpy as np
from jax import lax
from jax.experimental import pallas as pl
from jax.experimental.pallas import tpu as pltpu
from jax.sharding import PartitionSpec as P

LANES = 128
TOGETHER = 8
GROUP = 4
WIDE = jnp.float32
NARROW = jnp.bfloat16


def exchange_matrix():
    row = lax.broadcasted_iota(jnp.int32, (LANES, LANES), 0)
    col = lax.broadcasted_iota(jnp.int32, (LANES, LANES), 1)
    return (row + col == LANES - 1).astype(NARROW)


def gate_kernel(out_gate, in_gate, values, cotan, send):
    groups, per_group, _, owned, _ = send.shape
    mixed = (in_gate[...].astype(WIDE) * values[...].astype(WIDE)).astype(NARROW)
    gated = (cotan[...].astype(WIDE) * out_gate[...].astype(WIDE)).astype(NARROW)
    flipped = dot(gated.T, exchange_matrix()).astype(NARROW)
    for which, array in enumerate((mixed.T, flipped)):
        turned = array.reshape(per_group, groups, owned, LANES)
        for g in range(groups):
            send[g, :, which] = turned[:, g]


def gates(out_gate, in_gate, values, cotan, seq_count, chan_count):
    width = out_gate.shape[1]
    groups = chan_count
    per_group = seq_count // chan_count
    owned = width // seq_count
    steps = 2
    block = pl.BlockSpec((LANES, width // steps), lambda i: (0, i))
    return pl.pallas_call(
        gate_kernel,
        grid=(steps,),
        in_specs=[block] * 4,
        out_specs=pl.BlockSpec((groups, per_group // steps, 2, owned, LANES), lambda i: (0, i, 0, 0, 0)),
        out_shape=jax.ShapeDtypeStruct((groups, per_group, 2, owned, LANES), NARROW),
        cost_estimate=cost(2),
        name="gate_products",
    )(out_gate, in_gate, values, cotan)


def split(array):
    high = array.astype(NARROW)
    low = (array - high.astype(WIDE)).astype(NARROW)
    return high, low


def split_table(array):
    high = array.astype(NARROW)
    low = (array - high.astype(np.float64)).astype(NARROW)
    return high, low


def dft_tables(blocks):
    padded = LANES * LANES
    index = np.arange(LANES)
    angle = 2.0 * np.pi / LANES * (index[:, None] * index[None, :] % LANES)
    cos, sin = np.cos(angle), np.sin(angle)
    near_cos, near_sin = cos[:, :blocks], sin[:, :blocks]
    turn = 2.0 * np.pi / padded * (index[:, None] * index[None, :])

    def across(table, order):
        parts = split_table(table)
        return np.concatenate([parts[at] for at in order], axis=1)

    def down(table, order):
        parts = split_table(table)
        return np.concatenate([parts[at] for at in order], axis=0)

    return {
        "first": across(np.block([[near_cos, near_sin], [-near_sin, near_cos]]), (0, 1)),
        "first_real": across(np.block([[near_cos], [-near_sin]]), (0, 1)),
        "second": down(np.block([[cos, -sin], [sin, cos]]), (0, 0, 1)),
        "second_back": down(np.block([[cos, sin], [-sin, cos]]), (0, 0, 1)),
        "first_back": down(
            np.block([[near_cos.T, -near_sin.T], [near_sin.T, near_cos.T]]), (0, 1)
        ),
        "first_back_imag": down(np.block([[near_sin.T, near_cos.T]]), (0, 1)),
        "turn_cos": np.cos(turn).astype(np.float32),
        "turn_sin": np.sin(turn).astype(np.float32),
    }


def dot(left, right):
    return jnp.dot(left, right, preferred_element_type=WIDE)


def three_parts(real, imag):
    real_high, real_low = split(real)
    imag_high, imag_low = split(imag)
    return jnp.concatenate([real_high, imag_high, real_low, imag_low, real_high, imag_high], axis=1)


def grouped_dot(left, right):
    out = []
    for at in range(0, len(left), GROUP):
        group = left[at : at + GROUP]
        found = dot(jnp.concatenate(group, axis=0), right[...])
        out += [found[one * LANES : (one + 1) * LANES] for one in range(len(group))]
    return out


def spectra(data, first, second, turn_cos, turn_sin):
    stacked = jnp.concatenate([jnp.concatenate([one, one], axis=0) for one in data], axis=1)
    sections = dot(first[...], stacked)
    turned = []
    for at in range(len(data)):
        real = sections[:LANES, at * LANES : (at + 1) * LANES]
        imag = sections[LANES:, at * LANES : (at + 1) * LANES]
        turned_real = real * turn_cos[...] + imag * turn_sin[...]
        turned_imag = imag * turn_cos[...] - real * turn_sin[...]
        turned.append(three_parts(turned_real, turned_imag))
    found = grouped_dot(turned, second)
    return [found[at] for at in range(len(data))]


def sections_back(spectrum, second_back, turn_cos, turn_sin):
    parts = grouped_dot([three_parts(real, imag) for real, imag in spectrum], second_back)
    turned = []
    for at in range(len(spectrum)):
        real, imag = parts[at][:, :LANES], parts[at][:, LANES:]
        real_high, real_low = split(real * turn_cos[...] - imag * turn_sin[...])
        imag_high, imag_low = split(imag * turn_cos[...] + real * turn_sin[...])
        turned.append(
            (
                jnp.concatenate([real_high, imag_high], axis=0),
                jnp.concatenate([real_low, imag_low], axis=0),
            )
        )
    return turned


def signals(turned, first_back):
    rows = first_back.shape[0] // 2
    out = []
    for at in range(0, len(turned), 2):
        high = jnp.concatenate([one[0] for one in turned[at : at + 2]], axis=1)
        low = jnp.concatenate([one[1] for one in turned[at : at + 2]], axis=1)
        both = dot(first_back[...], high)
        result = both[:rows] + both[rows:] + dot(first_back[pl.ds(0, rows), :], low)
        out += [result[:, :LANES], result[:, LANES:]]
    return out


def spectrum_kernel(filters, first, second, turn_cos, turn_sin, spectrum, taps):
    owned = filters.shape[0]
    blocks = filters.shape[1] // LANES
    for q in range(blocks):
        taps[pl.ds(q * owned, owned), :] = filters[:, pl.ds(q * LANES, LANES)].astype(WIDE)

    def pair(at, carry):
        data = [
            taps[pl.ds(TOGETHER * at + c, blocks, stride=owned), :].astype(NARROW)
            for c in range(TOGETHER)
        ]
        found = spectra(data, first, second, turn_cos, turn_sin)
        for c in range(TOGETHER):
            spectrum[TOGETHER * at + c] = found[c]
        return carry

    lax.fori_loop(0, owned // TOGETHER, pair, 0)


def power_of_two(size):
    exponent = jnp.floor(jnp.log2(jnp.maximum(size, 1e-30)))
    down = jnp.exp2(-exponent).astype(NARROW).astype(WIDE)
    up = jnp.exp2(exponent).astype(NARROW).astype(WIDE)
    return down, up


def convolution_kernel(
    scale,
    received,
    spectrum_far,
    first,
    second,
    first_back,
    second_back,
    turn_cos,
    turn_sin,
    first_back_imag,
    send_far,
    grad_filters,
    filter_spectrum,
    send,
    signal,
    back,
    grads,
    loaded,
    sent,
):
    blocks, _, owned, _ = received.shape
    load = pltpu.make_async_copy(spectrum_far, filter_spectrum, loaded)
    load.start()
    ups = []
    for which in range(2):
        size = jnp.zeros((owned, LANES), WIDE)
        for j in range(blocks):
            size = jnp.maximum(size, jnp.abs(received[j, which].astype(WIDE)))
        size = jnp.broadcast_to(jnp.max(size, axis=1, keepdims=True), (owned, LANES))
        down, up = power_of_two(size)
        ups.append(up)
        for j in range(blocks):
            at = j if which == 0 else blocks - 1 - j
            signal[which, pl.ds(at * owned, owned), :] = received[j, which].astype(WIDE) * down
    load.wait()

    def pair(at, carry):
        data = []
        for c in range(TOGETHER):
            rows = [
                signal[which, pl.ds(TOGETHER * at + c, blocks, stride=owned), :].astype(NARROW)
                for which in range(2)
            ]
            data.append(jnp.concatenate(rows, axis=0))
        found = spectra(data, first, second, turn_cos, turn_sin)
        products = []
        squares = []
        for c in range(TOGETHER):
            real, imag = found[c][:, :LANES], found[c][:, LANES:]
            squares.append((0.5 * (real - imag) * (real + imag), real * imag))
            taps_real = filter_spectrum[TOGETHER * at + c, :, :LANES]
            taps_imag = filter_spectrum[TOGETHER * at + c, :, LANES:]
            products.append(
                (real * taps_real - imag * taps_imag, real * taps_imag + imag * taps_real)
            )
        turned = sections_back(products + squares, second_back, turn_cos, turn_sin)
        result = signals(turned[:TOGETHER], first_back)
        for c in range(TOGETHER):
            for which in range(2):
                back[which, pl.ds(TOGETHER * at + c, blocks, stride=owned), :] = result[c][
                    which * blocks : (which + 1) * blocks
                ]
        result = signals(turned[TOGETHER:], first_back_imag)
        for c in range(TOGETHER):
            grads[pl.ds(TOGETHER * at + c, blocks, stride=owned), :] = result[c]
        return carry

    lax.fori_loop(0, owned // TOGETHER, pair, 0)
    up = ups[0] * ups[1] * scale
    for j in range(blocks):
        grad_filters[j] = (grads[pl.ds(j * owned, owned), :] * up).astype(NARROW)
    up = [one * scale for one in ups]
    pieces = 4
    rows = blocks // pieces
    sends = []
    for piece in range(pieces):
        for at in range(piece * rows, (piece + 1) * rows):
            for which in range(2):
                j = at if which == 0 else blocks - 1 - at
                value = back[which, pl.ds(j * owned, owned), :] * up[which]
                send[at, which] = value.astype(NARROW)
        part = pl.ds(piece * rows, rows)
        sends.append(pltpu.make_async_copy(send.at[part], send_far.at[part], sent.at[piece]))
        sends[-1].start()
    for one in sends:
        one.wait()


def in_vmem(count):
    return [pl.BlockSpec(memory_space=pltpu.VMEM)] * count


def params(mebibytes=60):
    return pltpu.CompilerParams(vmem_limit_bytes=mebibytes * 1024 * 1024)


def cost(micros):
    return pl.CostEstimate(flops=int(micros * 1e9), bytes_accessed=1024, transcendentals=0)


def filter_spectra(filters, tables):
    owned, length = filters.shape
    return pl.pallas_call(
        spectrum_kernel,
        in_specs=in_vmem(5),
        out_specs=in_vmem(1)[0],
        out_shape=jax.ShapeDtypeStruct((owned, LANES, 2 * LANES), WIDE),
        scratch_shapes=[pltpu.VMEM((length // LANES * owned, LANES), WIDE)],
        compiler_params=params(),
        cost_estimate=cost(12),
        name="filter_spectra",
    )(filters, tables["first_real"], tables["second"], tables["turn_cos"], tables["turn_sin"])


def convolutions(received, filter_spectrum, tables, scale):
    blocks, _, owned, _ = received.shape
    operands = (
        received,
        filter_spectrum,
        tables["first"],
        tables["second"],
        tables["first_back"],
        tables["second_back"],
        tables["turn_cos"],
        tables["turn_sin"],
        tables["first_back_imag"],
    )
    far = pl.BlockSpec(memory_space=pl.ANY)
    return pl.pallas_call(
        functools.partial(convolution_kernel, scale / (LANES * LANES)),
        in_specs=in_vmem(1) + [far] + in_vmem(7),
        out_specs=[far] + in_vmem(1),
        out_shape=[
            jax.ShapeDtypeStruct(received.shape, NARROW),
            jax.ShapeDtypeStruct((blocks, owned, LANES), NARROW),
        ],
        scratch_shapes=[
            pltpu.VMEM(filter_spectrum.shape, WIDE),
            pltpu.VMEM(received.shape, NARROW),
            pltpu.VMEM((2, blocks * owned, LANES), WIDE),
            pltpu.VMEM((2, blocks * owned, LANES), WIDE),
            pltpu.VMEM((blocks * owned, LANES), WIDE),
            pltpu.SemaphoreType.DMA,
            pltpu.SemaphoreType.DMA((4,)),
        ],
        compiler_params=params(50),
        cost_estimate=cost(6),
        name="convolutions",
    )(*operands)


def result_kernel(out_gate, in_gate, values, cotan, received, output, grad_out, grad_in, grad_values):
    groups, per_group, _, owned, _ = received.shape
    turned = []
    for which in range(2):
        pieces = [received[g, :, which] for g in range(groups)]
        turned.append(jnp.stack(pieces, axis=1).reshape(groups * per_group * owned, LANES))
    conv = turned[0].T.astype(WIDE)
    grad_mixed = dot(turned[1], exchange_matrix()).astype(NARROW).T.astype(WIDE)
    output[...] = (out_gate[...].astype(WIDE) * conv).astype(NARROW)
    grad_out[...] = (cotan[...].astype(WIDE) * conv).astype(NARROW)
    grad_in[...] = (grad_mixed * values[...].astype(WIDE)).astype(NARROW)
    grad_values[...] = (grad_mixed * in_gate[...].astype(WIDE)).astype(NARROW)


def results(out_gate, in_gate, values, cotan, received):
    groups, per_group, _, owned, _ = received.shape
    width = out_gate.shape[1]
    steps = 2
    block = pl.BlockSpec((LANES, width // steps), lambda i: (0, i))
    return pl.pallas_call(
        result_kernel,
        grid=(steps,),
        in_specs=[block] * 4
        + [pl.BlockSpec((groups, per_group // steps, 2, owned, LANES), lambda i: (0, i, 0, 0, 0))],
        out_specs=[block] * 4,
        out_shape=[jax.ShapeDtypeStruct(out_gate.shape, NARROW)] * 4,
        compiler_params=params(50),
        cost_estimate=cost(2),
        name="gate_results",
    )(out_gate, in_gate, values, cotan, received)


def filter_kernel(received, grad_filters):
    blocks, owned, _ = received.shape
    flat = received[...].reshape(blocks * owned, LANES)
    flipped = dot(flat, exchange_matrix()).reshape(blocks, owned, LANES)
    for j in range(blocks):
        grad_filters[:, pl.ds(j * LANES, LANES)] = flipped[blocks - 1 - j]


def filter_results(received):
    blocks, owned, _ = received.shape
    return pl.pallas_call(
        filter_kernel,
        out_shape=jax.ShapeDtypeStruct((owned, blocks * LANES), WIDE),
        compiler_params=params(50),
        cost_estimate=cost(12),
        name="filter_results",
    )(received)


def per_device(output_gate, input_gate, values_in, filters, cotangent):
    seq_count = lax.axis_size("seq")
    chan_count = lax.axis_size("ch")
    per_group = seq_count // chan_count
    length, owned = filters.shape
    scale = 1.0 / math.sqrt(length)
    swap = []
    for s in range(seq_count):
        for c in range(chan_count):
            high, low = divmod(s, per_group)
            swap.append((s * chan_count + c, (c * per_group + low) * chan_count + high))
    tables = {name: jnp.asarray(table) for name, table in dft_tables(seq_count).items()}
    send = gates(output_gate, input_gate, values_in, cotangent, seq_count, chan_count)
    filters_owned, send = lax.optimization_barrier((filters.T, send))
    filters_here = lax.ppermute(filters_owned, ("seq", "ch"), swap)
    filter_spectrum = filter_spectra(filters_here, tables)
    sections = send.reshape(seq_count, 2, owned, LANES)
    received = lax.all_to_all(sections, "seq", split_axis=0, concat_axis=0, tiled=True)
    back, grads = convolutions(received, filter_spectrum, tables, scale)
    grads_owned = lax.ppermute(grads, ("seq", "ch"), swap)
    returned = lax.all_to_all(back, "seq", split_axis=0, concat_axis=0, tiled=True)
    returned = returned.reshape(chan_count, per_group, 2, owned, LANES)
    grad_filters = filter_results(grads_owned).T
    output, grad_out, grad_in, grad_values = results(
        output_gate, input_gate, values_in, cotangent, returned
    )
    return (output, grad_out, grad_in, grad_values, grad_filters)


def solution(mesh):
    by_position = P("seq", "ch")
    by_channel = P(None, ("seq", "ch"))
    return jax.shard_map(
        per_device,
        mesh=mesh,
        in_specs=(by_position, by_position, by_position, by_channel, by_position),
        out_specs=(by_position, by_position, by_position, by_position, by_channel),
        check_vma=False,
    )
```

```python
import functools
import math

import jax
import jax.numpy as jnp
import numpy as np
from jax import lax
from jax.experimental import pallas as pl
from jax.experimental.pallas import tpu as pltpu
from jax.sharding import PartitionSpec as P

LANES = 128
TOGETHER = 8
GROUP = 4
WIDE = jnp.float32
NARROW = jnp.bfloat16


def exchange_matrix():
    row = lax.broadcasted_iota(jnp.int32, (LANES, LANES), 0)
    col = lax.broadcasted_iota(jnp.int32, (LANES, LANES), 1)
    return (row + col == LANES - 1).astype(NARROW)


def gate_kernel(out_gate, in_gate, values, cotan, send):
    groups, per_group, _, owned, _ = send.shape
    mixed = (in_gate[...].astype(WIDE) * values[...].astype(WIDE)).astype(NARROW)
    gated = (cotan[...].astype(WIDE) * out_gate[...].astype(WIDE)).astype(NARROW)
    flipped = dot(gated.T, exchange_matrix()).astype(NARROW)
    for which, array in enumerate((mixed.T, flipped)):
        turned = array.reshape(per_group, groups, owned, LANES)
        for g in range(groups):
            send[g, :, which] = turned[:, g]


def gates(out_gate, in_gate, values, cotan, seq_count, chan_count):
    width = out_gate.shape[1]
    groups = chan_count
    per_group = seq_count // chan_count
    owned = width // seq_count
    steps = 2
    block = pl.BlockSpec((LANES, width // steps), lambda i: (0, i))
    return pl.pallas_call(
        gate_kernel,
        grid=(steps,),
        in_specs=[block] * 4,
        out_specs=pl.BlockSpec((groups, per_group // steps, 2, owned, LANES), lambda i: (0, i, 0, 0, 0)),
        out_shape=jax.ShapeDtypeStruct((groups, per_group, 2, owned, LANES), NARROW),
        cost_estimate=cost(2),
        name="gate_products",
    )(out_gate, in_gate, values, cotan)


def split(array):
    high = array.astype(NARROW)
    low = (array - high.astype(WIDE)).astype(NARROW)
    return high, low


def split_table(array):
    high = array.astype(NARROW)
    low = (array - high.astype(np.float64)).astype(NARROW)
    return high, low


def dft_tables(blocks):
    padded = LANES * LANES
    index = np.arange(LANES)
    angle = 2.0 * np.pi / LANES * (index[:, None] * index[None, :] % LANES)
    cos, sin = np.cos(angle), np.sin(angle)
    near_cos, near_sin = cos[:, :blocks], sin[:, :blocks]
    turn = 2.0 * np.pi / padded * (index[:, None] * index[None, :])

    def across(table, order):
        parts = split_table(table)
        return np.concatenate([parts[at] for at in order], axis=1)

    def down(table, order):
        parts = split_table(table)
        return np.concatenate([parts[at] for at in order], axis=0)

    return {
        "first": across(np.block([[near_cos, near_sin], [-near_sin, near_cos]]), (0, 1)),
        "first_real": across(np.block([[near_cos], [-near_sin]]), (0, 1)),
        "second": down(np.block([[cos, -sin], [sin, cos]]), (0, 0, 1)),
        "second_back": down(np.block([[cos, sin], [-sin, cos]]), (0, 0, 1)),
        "first_back": down(
            np.block([[near_cos.T, -near_sin.T], [near_sin.T, near_cos.T]]), (0, 1)
        ),
        "first_back_imag": down(np.block([[near_sin.T, near_cos.T]]), (0, 1)),
        "turn_cos": np.cos(turn).astype(np.float32),
        "turn_sin": np.sin(turn).astype(np.float32),
    }


def dot(left, right):
    return jnp.dot(left, right, preferred_element_type=WIDE)


def three_parts(real, imag):
    real_high, real_low = split(real)
    imag_high, imag_low = split(imag)
    return jnp.concatenate([real_high, imag_high, real_low, imag_low, real_high, imag_high], axis=1)


def grouped_dot(left, right):
    out = []
    for at in range(0, len(left), GROUP):
        group = left[at : at + GROUP]
        found = dot(jnp.concatenate(group, axis=0), right[...])
        out += [found[one * LANES : (one + 1) * LANES] for one in range(len(group))]
    return out


def spectra(data, first, second, turn_cos, turn_sin):
    stacked = jnp.concatenate([jnp.concatenate([one, one], axis=0) for one in data], axis=1)
    sections = dot(first[...], stacked)
    turned = []
    for at in range(len(data)):
        real = sections[:LANES, at * LANES : (at + 1) * LANES]
        imag = sections[LANES:, at * LANES : (at + 1) * LANES]
        turned_real = real * turn_cos[...] + imag * turn_sin[...]
        turned_imag = imag * turn_cos[...] - real * turn_sin[...]
        turned.append(three_parts(turned_real, turned_imag))
    found = grouped_dot(turned, second)
    return [found[at] for at in range(len(data))]


def sections_back(spectrum, second_back, turn_cos, turn_sin):
    parts = grouped_dot([three_parts(real, imag) for real, imag in spectrum], second_back)
    turned = []
    for at in range(len(spectrum)):
        real, imag = parts[at][:, :LANES], parts[at][:, LANES:]
        real_high, real_low = split(real * turn_cos[...] - imag * turn_sin[...])
        imag_high, imag_low = split(imag * turn_cos[...] + real * turn_sin[...])
        turned.append(
            (
                jnp.concatenate([real_high, imag_high], axis=0),
                jnp.concatenate([real_low, imag_low], axis=0),
            )
        )
    return turned


def signals(turned, first_back):
    rows = first_back.shape[0] // 2
    out = []
    for at in range(0, len(turned), 2):
        high = jnp.concatenate([one[0] for one in turned[at : at + 2]], axis=1)
        low = jnp.concatenate([one[1] for one in turned[at : at + 2]], axis=1)
        both = dot(first_back[...], high)
        result = both[:rows] + both[rows:] + dot(first_back[pl.ds(0, rows), :], low)
        out += [result[:, :LANES], result[:, LANES:]]
    return out


def spectrum_kernel(filters, first, second, turn_cos, turn_sin, spectrum, taps):
    owned = filters.shape[0]
    blocks = filters.shape[1] // LANES
    for q in range(blocks):
        taps[pl.ds(q * owned, owned), :] = filters[:, pl.ds(q * LANES, LANES)].astype(WIDE)

    def pair(at, carry):
        data = [
            taps[pl.ds(TOGETHER * at + c, blocks, stride=owned), :].astype(NARROW)
            for c in range(TOGETHER)
        ]
        found = spectra(data, first, second, turn_cos, turn_sin)
        for c in range(TOGETHER):
            spectrum[TOGETHER * at + c] = found[c]
        return carry

    lax.fori_loop(0, owned // TOGETHER, pair, 0)


def power_of_two(size):
    exponent = jnp.floor(jnp.log2(jnp.maximum(size, 1e-30)))
    down = jnp.exp2(-exponent).astype(NARROW).astype(WIDE)
    up = jnp.exp2(exponent).astype(NARROW).astype(WIDE)
    return down, up


def convolution_kernel(
    scale,
    received,
    spectrum_far,
    first,
    second,
    first_back,
    second_back,
    turn_cos,
    turn_sin,
    first_back_imag,
    send_far,
    grad_filters,
    filter_spectrum,
    send,
    signal,
    back,
    grads,
    loaded,
    sent,
):
    blocks, _, owned, _ = received.shape

    def load(at):
        rows = pl.ds(TOGETHER * at, TOGETHER)
        return pltpu.make_async_copy(spectrum_far.at[rows], filter_spectrum.at[rows], loaded.at[at])

    for at in range(owned // TOGETHER):
        load(at).start()
    ups = []
    for which in range(2):
        size = jnp.zeros((owned, LANES), WIDE)
        for j in range(blocks):
            size = jnp.maximum(size, jnp.abs(received[j, which].astype(WIDE)))
        size = jnp.broadcast_to(jnp.max(size, axis=1, keepdims=True), (owned, LANES))
        down, up = power_of_two(size)
        ups.append(up)
        for j in range(blocks):
            at = j if which == 0 else blocks - 1 - j
            signal[which, pl.ds(at * owned, owned), :] = received[j, which].astype(WIDE) * down

    def pair(at, carry):
        load(at).wait()
        data = []
        for c in range(TOGETHER):
            rows = [
                signal[which, pl.ds(TOGETHER * at + c, blocks, stride=owned), :].astype(NARROW)
                for which in range(2)
            ]
            data.append(jnp.concatenate(rows, axis=0))
        found = spectra(data, first, second, turn_cos, turn_sin)
        products = []
        squares = []
        for c in range(TOGETHER):
            real, imag = found[c][:, :LANES], found[c][:, LANES:]
            squares.append((0.5 * (real - imag) * (real + imag), real * imag))
            taps_real = filter_spectrum[TOGETHER * at + c, :, :LANES]
            taps_imag = filter_spectrum[TOGETHER * at + c, :, LANES:]
            products.append(
                (real * taps_real - imag * taps_imag, real * taps_imag + imag * taps_real)
            )
        turned = sections_back(products + squares, second_back, turn_cos, turn_sin)
        result = signals(turned[:TOGETHER], first_back)
        for c in range(TOGETHER):
            for which in range(2):
                back[which, pl.ds(TOGETHER * at + c, blocks, stride=owned), :] = result[c][
                    which * blocks : (which + 1) * blocks
                ]
        result = signals(turned[TOGETHER:], first_back_imag)
        for c in range(TOGETHER):
            grads[pl.ds(TOGETHER * at + c, blocks, stride=owned), :] = result[c]
        return carry

    lax.fori_loop(0, owned // TOGETHER, pair, 0)
    up = ups[0] * ups[1] * scale
    for j in range(blocks):
        grad_filters[j] = (grads[pl.ds(j * owned, owned), :] * up).astype(NARROW)
    up = [one * scale for one in ups]
    pieces = 4
    rows = blocks // pieces
    sends = []
    for piece in range(pieces):
        for at in range(piece * rows, (piece + 1) * rows):
            for which in range(2):
                j = at if which == 0 else blocks - 1 - at
                value = back[which, pl.ds(j * owned, owned), :] * up[which]
                send[at, which] = value.astype(NARROW)
        part = pl.ds(piece * rows, rows)
        sends.append(pltpu.make_async_copy(send.at[part], send_far.at[part], sent.at[piece]))
        sends[-1].start()
    for one in sends:
        one.wait()


def in_vmem(count):
    return [pl.BlockSpec(memory_space=pltpu.VMEM)] * count


def params(mebibytes=60):
    return pltpu.CompilerParams(vmem_limit_bytes=mebibytes * 1024 * 1024)


def cost(micros):
    return pl.CostEstimate(flops=int(micros * 1e9), bytes_accessed=1024, transcendentals=0)


def filter_spectra(filters, tables):
    owned, length = filters.shape
    return pl.pallas_call(
        spectrum_kernel,
        in_specs=in_vmem(5),
        out_specs=in_vmem(1)[0],
        out_shape=jax.ShapeDtypeStruct((owned, LANES, 2 * LANES), WIDE),
        scratch_shapes=[pltpu.VMEM((length // LANES * owned, LANES), WIDE)],
        compiler_params=params(),
        cost_estimate=cost(12),
        name="filter_spectra",
    )(filters, tables["first_real"], tables["second"], tables["turn_cos"], tables["turn_sin"])


def convolutions(received, filter_spectrum, tables, scale):
    blocks, _, owned, _ = received.shape
    operands = (
        received,
        filter_spectrum,
        tables["first"],
        tables["second"],
        tables["first_back"],
        tables["second_back"],
        tables["turn_cos"],
        tables["turn_sin"],
        tables["first_back_imag"],
    )
    far = pl.BlockSpec(memory_space=pl.ANY)
    return pl.pallas_call(
        functools.partial(convolution_kernel, scale / (LANES * LANES)),
        in_specs=in_vmem(1) + [far] + in_vmem(7),
        out_specs=[far] + in_vmem(1),
        out_shape=[
            jax.ShapeDtypeStruct(received.shape, NARROW),
            jax.ShapeDtypeStruct((blocks, owned, LANES), NARROW),
        ],
        scratch_shapes=[
            pltpu.VMEM(filter_spectrum.shape, WIDE),
            pltpu.VMEM(received.shape, NARROW),
            pltpu.VMEM((2, blocks * owned, LANES), WIDE),
            pltpu.VMEM((2, blocks * owned, LANES), WIDE),
            pltpu.VMEM((blocks * owned, LANES), WIDE),
            pltpu.SemaphoreType.DMA((owned // TOGETHER,)),
            pltpu.SemaphoreType.DMA((4,)),
        ],
        compiler_params=params(50),
        cost_estimate=cost(6),
        name="convolutions",
    )(*operands)


def result_kernel(out_gate, in_gate, values, cotan, received, output, grad_out, grad_in, grad_values):
    groups, per_group, _, owned, _ = received.shape
    turned = []
    for which in range(2):
        pieces = [received[g, :, which] for g in range(groups)]
        turned.append(jnp.stack(pieces, axis=1).reshape(groups * per_group * owned, LANES))
    conv = turned[0].T.astype(WIDE)
    grad_mixed = dot(turned[1], exchange_matrix()).astype(NARROW).T.astype(WIDE)
    output[...] = (out_gate[...].astype(WIDE) * conv).astype(NARROW)
    grad_out[...] = (cotan[...].astype(WIDE) * conv).astype(NARROW)
    grad_in[...] = (grad_mixed * values[...].astype(WIDE)).astype(NARROW)
    grad_values[...] = (grad_mixed * in_gate[...].astype(WIDE)).astype(NARROW)


def results(out_gate, in_gate, values, cotan, received):
    groups, per_group, _, owned, _ = received.shape
    width = out_gate.shape[1]
    steps = 2
    block = pl.BlockSpec((LANES, width // steps), lambda i: (0, i))
    return pl.pallas_call(
        result_kernel,
        grid=(steps,),
        in_specs=[block] * 4
        + [pl.BlockSpec((groups, per_group // steps, 2, owned, LANES), lambda i: (0, i, 0, 0, 0))],
        out_specs=[block] * 4,
        out_shape=[jax.ShapeDtypeStruct(out_gate.shape, NARROW)] * 4,
        compiler_params=params(50),
        cost_estimate=cost(2),
        name="gate_results",
    )(out_gate, in_gate, values, cotan, received)


def filter_kernel(received, grad_filters):
    blocks, owned, _ = received.shape
    flat = received[...].reshape(blocks * owned, LANES)
    flipped = dot(flat, exchange_matrix()).reshape(blocks, owned, LANES)
    for j in range(blocks):
        grad_filters[:, pl.ds(j * LANES, LANES)] = flipped[blocks - 1 - j]


def filter_results(received):
    blocks, owned, _ = received.shape
    return pl.pallas_call(
        filter_kernel,
        out_shape=jax.ShapeDtypeStruct((owned, blocks * LANES), WIDE),
        compiler_params=params(50),
        cost_estimate=cost(12),
        name="filter_results",
    )(received)


def per_device(output_gate, input_gate, values_in, filters, cotangent):
    seq_count = lax.axis_size("seq")
    chan_count = lax.axis_size("ch")
    per_group = seq_count // chan_count
    length, owned = filters.shape
    scale = 1.0 / math.sqrt(length)
    swap = []
    for s in range(seq_count):
        for c in range(chan_count):
            high, low = divmod(s, per_group)
            swap.append((s * chan_count + c, (c * per_group + low) * chan_count + high))
    tables = {name: jnp.asarray(table) for name, table in dft_tables(seq_count).items()}
    send = gates(output_gate, input_gate, values_in, cotangent, seq_count, chan_count)
    filters_owned, send = lax.optimization_barrier((filters.T, send))
    filters_here = lax.ppermute(filters_owned, ("seq", "ch"), swap)
    filter_spectrum = filter_spectra(filters_here, tables)
    sections = send.reshape(seq_count, 2, owned, LANES)
    received = lax.all_to_all(sections, "seq", split_axis=0, concat_axis=0, tiled=True)
    back, grads = convolutions(received, filter_spectrum, tables, scale)
    grads_owned = lax.ppermute(grads, ("seq", "ch"), swap)
    returned = lax.all_to_all(back, "seq", split_axis=0, concat_axis=0, tiled=True)
    returned = returned.reshape(chan_count, per_group, 2, owned, LANES)
    output, grad_out, grad_in, grad_values = results(
        output_gate, input_gate, values_in, cotangent, returned
    )
    grads_owned, output = lax.optimization_barrier((grads_owned, output))
    grad_filters = filter_results(grads_owned).T
    return (output, grad_out, grad_in, grad_values, grad_filters)


def solution(mesh):
    by_position = P("seq", "ch")
    by_channel = P(None, ("seq", "ch"))
    return jax.shard_map(
        per_device,
        mesh=mesh,
        in_specs=(by_position, by_position, by_position, by_channel, by_position),
        out_specs=(by_position, by_position, by_position, by_position, by_channel),
        check_vma=False,
    )
```

```python
import functools
import math

import jax
import jax.numpy as jnp
import numpy as np
from jax import lax
from jax.experimental import pallas as pl
from jax.experimental.pallas import tpu as pltpu
from jax.sharding import PartitionSpec as P

LANES = 128
TOGETHER = 8
GROUP = 4
PARTS = 2
WIDE = jnp.float32
NARROW = jnp.bfloat16


def exchange_matrix():
    row = lax.broadcasted_iota(jnp.int32, (LANES, LANES), 0)
    col = lax.broadcasted_iota(jnp.int32, (LANES, LANES), 1)
    return (row + col == LANES - 1).astype(NARROW)


def gate_kernel(out_gate, in_gate, values, cotan, send):
    groups, per_group, _, owned, _ = send.shape
    mixed = (in_gate[...].astype(WIDE) * values[...].astype(WIDE)).astype(NARROW)
    gated = (cotan[...].astype(WIDE) * out_gate[...].astype(WIDE)).astype(NARROW)
    flipped = dot(gated.T, exchange_matrix()).astype(NARROW)
    for which, array in enumerate((mixed.T, flipped)):
        turned = array.reshape(per_group, groups, owned, LANES)
        for g in range(groups):
            send[g, :, which] = turned[:, g]


def gates(out_gate, in_gate, values, cotan, seq_count, chan_count):
    width = out_gate.shape[1]
    groups = chan_count
    per_group = seq_count // chan_count
    owned = width // seq_count
    steps = 2
    block = pl.BlockSpec((LANES, width // steps), lambda i: (0, i))
    return pl.pallas_call(
        gate_kernel,
        grid=(steps,),
        in_specs=[block] * 4,
        out_specs=pl.BlockSpec((groups, per_group // steps, 2, owned, LANES), lambda i: (0, i, 0, 0, 0)),
        out_shape=jax.ShapeDtypeStruct((groups, per_group, 2, owned, LANES), NARROW),
        cost_estimate=cost(2),
        name="gate_products",
    )(out_gate, in_gate, values, cotan)


def split(array):
    high = array.astype(NARROW)
    low = (array - high.astype(WIDE)).astype(NARROW)
    return high, low


def split_table(array):
    high = array.astype(NARROW)
    low = (array - high.astype(np.float64)).astype(NARROW)
    return high, low


def dft_tables(blocks):
    padded = LANES * LANES
    index = np.arange(LANES)
    angle = 2.0 * np.pi / LANES * (index[:, None] * index[None, :] % LANES)
    cos, sin = np.cos(angle), np.sin(angle)
    near_cos, near_sin = cos[:, :blocks], sin[:, :blocks]
    turn = 2.0 * np.pi / padded * (index[:, None] * index[None, :])

    def across(table, order):
        parts = split_table(table)
        return np.concatenate([parts[at] for at in order], axis=1)

    def down(table, order):
        parts = split_table(table)
        return np.concatenate([parts[at] for at in order], axis=0)

    return {
        "first": across(np.block([[near_cos, near_sin], [-near_sin, near_cos]]), (0, 1)),
        "first_real": across(np.block([[near_cos], [-near_sin]]), (0, 1)),
        "second": down(np.block([[cos, -sin], [sin, cos]]), (0, 0, 1)),
        "second_back": down(np.block([[cos, sin], [-sin, cos]]), (0, 0, 1)),
        "first_back": down(
            np.block([[near_cos.T, -near_sin.T], [near_sin.T, near_cos.T]]), (0, 1)
        ),
        "first_back_imag": down(np.block([[near_sin.T, near_cos.T]]), (0, 1)),
        "turn_cos": np.cos(turn).astype(np.float32),
        "turn_sin": np.sin(turn).astype(np.float32),
    }


def dot(left, right):
    return jnp.dot(left, right, preferred_element_type=WIDE)


def three_parts(real, imag):
    real_high, real_low = split(real)
    imag_high, imag_low = split(imag)
    return jnp.concatenate([real_high, imag_high, real_low, imag_low, real_high, imag_high], axis=1)


def grouped_dot(left, right):
    out = []
    for at in range(0, len(left), GROUP):
        group = left[at : at + GROUP]
        found = dot(jnp.concatenate(group, axis=0), right[...])
        out += [found[one * LANES : (one + 1) * LANES] for one in range(len(group))]
    return out


def spectra(data, first, second, turn_cos, turn_sin):
    stacked = jnp.concatenate([jnp.concatenate([one, one], axis=0) for one in data], axis=1)
    sections = dot(first[...], stacked)
    turned = []
    for at in range(len(data)):
        real = sections[:LANES, at * LANES : (at + 1) * LANES]
        imag = sections[LANES:, at * LANES : (at + 1) * LANES]
        turned_real = real * turn_cos[...] + imag * turn_sin[...]
        turned_imag = imag * turn_cos[...] - real * turn_sin[...]
        turned.append(three_parts(turned_real, turned_imag))
    found = grouped_dot(turned, second)
    return [found[at] for at in range(len(data))]


def sections_back(spectrum, second_back, turn_cos, turn_sin):
    parts = grouped_dot([three_parts(real, imag) for real, imag in spectrum], second_back)
    turned = []
    for at in range(len(spectrum)):
        real, imag = parts[at][:, :LANES], parts[at][:, LANES:]
        real_high, real_low = split(real * turn_cos[...] - imag * turn_sin[...])
        imag_high, imag_low = split(imag * turn_cos[...] + real * turn_sin[...])
        turned.append(
            (
                jnp.concatenate([real_high, imag_high], axis=0),
                jnp.concatenate([real_low, imag_low], axis=0),
            )
        )
    return turned


def signals(turned, first_back):
    rows = first_back.shape[0] // 2
    out = []
    for at in range(0, len(turned), 2):
        high = jnp.concatenate([one[0] for one in turned[at : at + 2]], axis=1)
        low = jnp.concatenate([one[1] for one in turned[at : at + 2]], axis=1)
        both = dot(first_back[...], high)
        result = both[:rows] + both[rows:] + dot(first_back[pl.ds(0, rows), :], low)
        out += [result[:, :LANES], result[:, LANES:]]
    return out


def spectrum_kernel(filters, first, second, turn_cos, turn_sin, spectrum, taps):
    owned = filters.shape[0]
    blocks = filters.shape[1] // LANES
    for q in range(blocks):
        taps[pl.ds(q * owned, owned), :] = filters[:, pl.ds(q * LANES, LANES)].astype(WIDE)

    def pair(at, carry):
        data = [
            taps[pl.ds(TOGETHER * at + c, blocks, stride=owned), :].astype(NARROW)
            for c in range(TOGETHER)
        ]
        found = spectra(data, first, second, turn_cos, turn_sin)
        for c in range(TOGETHER):
            spectrum[TOGETHER * at + c] = found[c]
        return carry

    lax.fori_loop(0, owned // TOGETHER, pair, 0)


def power_of_two(size):
    exponent = jnp.floor(jnp.log2(jnp.maximum(size, 1e-30)))
    down = jnp.exp2(-exponent).astype(NARROW).astype(WIDE)
    up = jnp.exp2(exponent).astype(NARROW).astype(WIDE)
    return down, up


def convolution_kernel(
    scale,
    received,
    spectrum_far,
    first,
    second,
    first_back,
    second_back,
    turn_cos,
    turn_sin,
    first_back_imag,
    send_far,
    *others,
):
    grad_filters = others[:PARTS]
    filter_spectrum, send, signal, back, grads, loaded, sent = others[PARTS:]
    blocks, _, owned, _ = received.shape

    def load(at):
        rows = pl.ds(TOGETHER * at, TOGETHER)
        return pltpu.make_async_copy(spectrum_far.at[rows], filter_spectrum.at[rows], loaded.at[at])

    for at in range(owned // TOGETHER):
        load(at).start()
    ups = []
    for which in range(2):
        size = jnp.zeros((owned, LANES), WIDE)
        for j in range(blocks):
            size = jnp.maximum(size, jnp.abs(received[j, which].astype(WIDE)))
        size = jnp.broadcast_to(jnp.max(size, axis=1, keepdims=True), (owned, LANES))
        down, up = power_of_two(size)
        ups.append(up)
        for j in range(blocks):
            at = j if which == 0 else blocks - 1 - j
            signal[which, pl.ds(at * owned, owned), :] = received[j, which].astype(WIDE) * down

    def pair(at, carry):
        load(at).wait()
        data = []
        for c in range(TOGETHER):
            rows = [
                signal[which, pl.ds(TOGETHER * at + c, blocks, stride=owned), :].astype(NARROW)
                for which in range(2)
            ]
            data.append(jnp.concatenate(rows, axis=0))
        found = spectra(data, first, second, turn_cos, turn_sin)
        products = []
        squares = []
        for c in range(TOGETHER):
            real, imag = found[c][:, :LANES], found[c][:, LANES:]
            squares.append((0.5 * (real - imag) * (real + imag), real * imag))
            taps_real = filter_spectrum[TOGETHER * at + c, :, :LANES]
            taps_imag = filter_spectrum[TOGETHER * at + c, :, LANES:]
            products.append(
                (real * taps_real - imag * taps_imag, real * taps_imag + imag * taps_real)
            )
        turned = sections_back(products + squares, second_back, turn_cos, turn_sin)
        result = signals(turned[:TOGETHER], first_back)
        for c in range(TOGETHER):
            for which in range(2):
                back[which, pl.ds(TOGETHER * at + c, blocks, stride=owned), :] = result[c][
                    which * blocks : (which + 1) * blocks
                ]
        result = signals(turned[TOGETHER:], first_back_imag)
        for c in range(TOGETHER):
            grads[pl.ds(TOGETHER * at + c, blocks, stride=owned), :] = result[c]
        return carry

    lax.fori_loop(0, owned // TOGETHER, pair, 0)
    up = ups[0] * ups[1] * scale
    members = blocks // PARTS
    for j in range(blocks):
        value = grads[pl.ds(j * owned, owned), :] * up
        grad_filters[j // members][j % members] = value.astype(NARROW)
    up = [one * scale for one in ups]
    pieces = 4
    rows = blocks // pieces
    sends = []
    for piece in range(pieces):
        for at in range(piece * rows, (piece + 1) * rows):
            for which in range(2):
                j = at if which == 0 else blocks - 1 - at
                value = back[which, pl.ds(j * owned, owned), :] * up[which]
                send[at, which] = value.astype(NARROW)
        part = pl.ds(piece * rows, rows)
        sends.append(pltpu.make_async_copy(send.at[part], send_far.at[part], sent.at[piece]))
        sends[-1].start()
    for one in sends:
        one.wait()


def in_vmem(count):
    return [pl.BlockSpec(memory_space=pltpu.VMEM)] * count


def params(mebibytes=60):
    return pltpu.CompilerParams(vmem_limit_bytes=mebibytes * 1024 * 1024)


def cost(micros):
    return pl.CostEstimate(flops=int(micros * 1e9), bytes_accessed=1024, transcendentals=0)


def filter_spectra(filters, tables):
    owned, length = filters.shape
    return pl.pallas_call(
        spectrum_kernel,
        in_specs=in_vmem(5),
        out_specs=in_vmem(1)[0],
        out_shape=jax.ShapeDtypeStruct((owned, LANES, 2 * LANES), WIDE),
        scratch_shapes=[pltpu.VMEM((length // LANES * owned, LANES), WIDE)],
        compiler_params=params(),
        cost_estimate=cost(12),
        name="filter_spectra",
    )(filters, tables["first_real"], tables["second"], tables["turn_cos"], tables["turn_sin"])


def convolutions(received, filter_spectrum, tables, scale):
    blocks, _, owned, _ = received.shape
    operands = (
        received,
        filter_spectrum,
        tables["first"],
        tables["second"],
        tables["first_back"],
        tables["second_back"],
        tables["turn_cos"],
        tables["turn_sin"],
        tables["first_back_imag"],
    )
    far = pl.BlockSpec(memory_space=pl.ANY)
    return pl.pallas_call(
        functools.partial(convolution_kernel, scale / (LANES * LANES)),
        in_specs=in_vmem(1) + [far] + in_vmem(7),
        out_specs=[far] + in_vmem(PARTS),
        out_shape=[
            jax.ShapeDtypeStruct(received.shape, NARROW),
        ]
        + [jax.ShapeDtypeStruct((blocks // PARTS, owned, LANES), NARROW)] * PARTS,
        scratch_shapes=[
            pltpu.VMEM(filter_spectrum.shape, WIDE),
            pltpu.VMEM(received.shape, NARROW),
            pltpu.VMEM((2, blocks * owned, LANES), WIDE),
            pltpu.VMEM((2, blocks * owned, LANES), WIDE),
            pltpu.VMEM((blocks * owned, LANES), WIDE),
            pltpu.SemaphoreType.DMA((owned // TOGETHER,)),
            pltpu.SemaphoreType.DMA((4,)),
        ],
        compiler_params=params(50),
        cost_estimate=cost(6),
        name="convolutions",
    )(*operands)


def result_kernel(out_gate, in_gate, values, cotan, received, output, grad_out, grad_in, grad_values):
    groups, per_group, _, owned, _ = received.shape
    turned = []
    for which in range(2):
        pieces = [received[g, :, which] for g in range(groups)]
        turned.append(jnp.stack(pieces, axis=1).reshape(groups * per_group * owned, LANES))
    conv = turned[0].T.astype(WIDE)
    grad_mixed = dot(turned[1], exchange_matrix()).astype(NARROW).T.astype(WIDE)
    output[...] = (out_gate[...].astype(WIDE) * conv).astype(NARROW)
    grad_out[...] = (cotan[...].astype(WIDE) * conv).astype(NARROW)
    grad_in[...] = (grad_mixed * values[...].astype(WIDE)).astype(NARROW)
    grad_values[...] = (grad_mixed * in_gate[...].astype(WIDE)).astype(NARROW)


def results(out_gate, in_gate, values, cotan, received):
    groups, per_group, _, owned, _ = received.shape
    width = out_gate.shape[1]
    steps = 2
    block = pl.BlockSpec((LANES, width // steps), lambda i: (0, i))
    return pl.pallas_call(
        result_kernel,
        grid=(steps,),
        in_specs=[block] * 4
        + [pl.BlockSpec((groups, per_group // steps, 2, owned, LANES), lambda i: (0, i, 0, 0, 0))],
        out_specs=[block] * 4,
        out_shape=[jax.ShapeDtypeStruct(out_gate.shape, NARROW)] * 4,
        compiler_params=params(50),
        cost_estimate=cost(2),
        name="gate_results",
    )(out_gate, in_gate, values, cotan, received)


def filter_kernel(received, *refs):
    grad_filters = refs[-1]
    members, owned, _ = received.shape
    flat = received[...].reshape(members * owned, LANES)
    flipped = dot(flat, exchange_matrix()).reshape(members, owned, LANES)
    for j in range(members):
        grad_filters[:, pl.ds((members - 1 - j) * LANES, LANES)] = flipped[j]


def filter_results(received, part, so_far):
    members, owned, _ = received.shape
    width = members * LANES
    before = [] if so_far is None else [so_far]
    return pl.pallas_call(
        filter_kernel,
        grid=(1,),
        in_specs=[pl.BlockSpec(received.shape, lambda i: (0, 0, 0))]
        + [pl.BlockSpec(memory_space=pl.ANY)] * len(before),
        out_specs=pl.BlockSpec((owned, width), lambda i: (0, PARTS - 1 - part)),
        out_shape=jax.ShapeDtypeStruct((owned, PARTS * width), WIDE),
        input_output_aliases={1: 0} if before else {},
        compiler_params=params(50),
        cost_estimate=cost(2),
        name="filter_results",
    )(received, *before)


def per_device(output_gate, input_gate, values_in, filters, cotangent):
    seq_count = lax.axis_size("seq")
    chan_count = lax.axis_size("ch")
    per_group = seq_count // chan_count
    length, owned = filters.shape
    scale = 1.0 / math.sqrt(length)
    swap = []
    for s in range(seq_count):
        for c in range(chan_count):
            high, low = divmod(s, per_group)
            swap.append((s * chan_count + c, (c * per_group + low) * chan_count + high))
    tables = {name: jnp.asarray(table) for name, table in dft_tables(seq_count).items()}
    send = gates(output_gate, input_gate, values_in, cotangent, seq_count, chan_count)
    filters_owned, send = lax.optimization_barrier((filters.T, send))
    filters_here = lax.ppermute(filters_owned, ("seq", "ch"), swap)
    filter_spectrum = filter_spectra(filters_here, tables)
    sections = send.reshape(seq_count, 2, owned, LANES)
    received = lax.all_to_all(sections, "seq", split_axis=0, concat_axis=0, tiled=True)
    back, *grads = convolutions(received, filter_spectrum, tables, scale)
    grads_owned = [lax.ppermute(one, ("seq", "ch"), swap) for one in grads]
    returned = lax.all_to_all(back, "seq", split_axis=0, concat_axis=0, tiled=True)
    returned = returned.reshape(chan_count, per_group, 2, owned, LANES)
    output, grad_out, grad_in, grad_values = results(
        output_gate, input_gate, values_in, cotangent, returned
    )
    grads_owned[0], output = lax.optimization_barrier((grads_owned[0], output))
    grad_filters = None
    for part in range(PARTS):
        grad_filters = filter_results(grads_owned[part], part, grad_filters)
    grad_filters = grad_filters.T
    return (output, grad_out, grad_in, grad_values, grad_filters)


def solution(mesh):
    by_position = P("seq", "ch")
    by_channel = P(None, ("seq", "ch"))
    return jax.shard_map(
        per_device,
        mesh=mesh,
        in_specs=(by_position, by_position, by_position, by_channel, by_position),
        out_specs=(by_position, by_position, by_position, by_position, by_channel),
        check_vma=False,
    )
```
